1024 devices in a mesh: lon: 16 (over x, y), lat: 16 (over z_lo), comp: 4 (over z_hi, core).
Axes of the slice: x: 4, y: 4, z: 32 (z_hi: 2, z_lo: 16; z = z_hi * 16 + z_lo), core: 2. Of those that a mesh axis runs over, the one named last changes fastest.
Arguments:
- fields: float32 [4, 8, 768, 8192], P('comp', None, 'lat', 'lon'), may hold values from -6 to 6
- diffusion: float32 [4, 768, 8192], P('comp', 'lat', 'lon'), may hold values from 0.04 to 0.24
- exchange_coef: float32 [4, 768, 8192], P('comp', 'lat', 'lon'), may hold values from 0.2 to 1
- sea_seen: bfloat16 [768, 8192], P('lat', 'lon'), may hold values from -6 to 6
- remap_code: int32 [8, 768, 8192], P(None, 'lat', 'lon'), may hold values from 0 to 47
- remap_weight: float32 [8, 768, 8192], P(None, 'lat', 'lon'), may hold values from 0.05 to 0.25
- land_sea: int32 [768, 8192], P('lat', 'lon'), may hold values 0 or 1
- fold_partner: int32 [8192], replicated, may hold values from 0 to 8191, as said below
Outputs:
- updated: float32 [4, 8, 768, 8192], P('comp', None, 'lat', 'lon')
- contrast: float32 [4, 768, 8192], P('comp', 'lat', 'lon')
The draws below stay inside these ranges and needn't reach their ends.
Inputs may be any that keep to these rules, and one draw needn't show every extreme that they name: `remap_code`: codes name one of the 3 members and a cell of the 4 x 4 window as stated in the reference program. fold_partner[j] = (s - j) mod 8192 for one whole number s.
All inputs are finite; a program needn't handle non-finite values. No bound on the sum of `land_sea` on one device may be relied on, other than what follows from the above.
Results may differ from the reference program's by a relative error of at most 0.0021.
Values may be sent and summed in bfloat16 or wider, within the bound.
A program may use at most 32 MiB of HBM per device.

```python
import math
import jax
import jax.numpy as jnp

ROWS = 48
COLS = 512
SLICES = 8
SUBSTEPS = 2
TAPS = 8
WIN = 4
NY = 768
NX = 8192
N_COMP = 4


def draw_fold_partner(key, part):
    key = jax.random.fold_in(key, 7)
    offset = jax.random.randint(key, (), 0, NX, dtype=jnp.int32)
    columns = jnp.arange(NX, dtype=jnp.int32)
    return jnp.mod(offset - columns, NX).astype(jnp.int32)


def plant(array, own_key, low, largest):
    dims = array.shape
    place = [jax.random.randint(jax.random.fold_in(own_key, axis), (), 0, dims[axis]) for axis in range(len(dims))]
    array = array.at[tuple(place)].set(low)
    longest = dims.index(max(dims))
    place[longest] = (place[longest] + 1) % dims[longest]
    return array.at[tuple(place)].set(largest)


def block_scale(stream_key, extent, pieces, low, largest):
    gain, own = 1.0, jax.random.fold_in(stream_key, 6)
    for axis_at, shards_of in pieces:
        draws = jnp.exp(jax.random.uniform(jax.random.fold_in(own, axis_at), (shards_of,), jnp.float32, low / len(pieces), largest / len(pieces)))
        gain = gain * jnp.repeat(draws, extent[axis_at] // shards_of).reshape([-1 if axis == axis_at else 1 for axis in range(len(extent))])
    return gain


def normal_values(own_key, shape, deviation, most, cuts=(), kind=jnp.bfloat16):
    values = deviation * jax.random.normal(own_key, shape, jnp.float32)
    if cuts:
        values = values * block_scale(own_key, shape, cuts, -0.22, 0.18)
    return jnp.clip(values, -most, most).astype(kind)


def setup_inputs(seed: int = 0) -> dict:
    splits = jax.random.split(jax.random.key(seed), 9)
    return {
        "fields": normal_values(splits[0], (N_COMP, SLICES, NY, NX), 1.0, 6.0, ((0, 4), (2, 16), (3, 16)), jnp.float32),
        "diffusion": jnp.clip(0.04 + 0.19999999552965164 * jax.random.uniform(splits[1], (N_COMP, NY, NX), jnp.float32) ** block_scale(splits[1], (N_COMP, NY, NX), ((0, 4), (1, 16), (2, 16)), -0.2, 0.2), 0.04, 0.24),
        "exchange_coef": jnp.clip(jnp.exp(math.log(1.0) - 1.609438 * jax.random.uniform(splits[2], (N_COMP, NY, NX), jnp.float32) ** block_scale(splits[2], (N_COMP, NY, NX), ((0, 4), (1, 16), (2, 16)), -0.2, 0.2)), 0.2, 1.0),
        "sea_seen": normal_values(splits[3], (NY, NX), 1.0, 6.0, ((0, 16), (1, 16))),
        "remap_code": plant(jax.random.randint(splits[4], (TAPS, NY, NX), 0, (N_COMP - 1) * WIN * WIN), jax.random.fold_in(splits[4], 1), 0, ((N_COMP - 1) * WIN * WIN) - 1).astype(jnp.int32),
        "remap_weight": jnp.clip(0.05 + 0.2 * jax.random.uniform(splits[5], (TAPS, NY, NX), jnp.float32) ** block_scale(splits[5], (TAPS, NY, NX), ((1, 16), (2, 16)), -0.2, 0.2), 0.05, 0.25),
        "land_sea": plant((jax.random.randint(splits[6], (NY, NX), 0, 4) < 3).astype(jnp.int32), jax.random.fold_in(splits[6], 1), 0, 1),
        "fold_partner": draw_fold_partner(jax.random.fold_in(splits[8], 71), 0),
    }


air_gain = 0.5


def diffuse(current, rate_tile, fold_partner, folded):
    zero_row = jnp.zeros_like(current[:, :1, :])
    if folded:
        ghost_row = current[:, -1:, :][:, :, fold_partner]
    else:
        ghost_row = zero_row
    north_side = jnp.concatenate([current[:, 1:, :], ghost_row], axis=1)
    south_side = jnp.concatenate([zero_row, current[:, :-1, :]], axis=1)
    east_side = jnp.roll(current, -1, axis=2)
    west_side = jnp.roll(current, 1, axis=2)
    return current + rate_tile * (north_side + south_side + east_side + west_side - 4.0 * current)


def remap(air_flux, remap_code, remap_weight, land_sea):
    members = air_flux.shape[0]
    row_ids = jnp.arange(NY, dtype=jnp.int32)[None, :, None]
    col_ids = jnp.arange(NX, dtype=jnp.int32)[None, None, :]
    member = remap_code // (WIN * WIN)
    row_shift = (remap_code // WIN) % WIN - 1
    col_shift = remap_code % WIN - 1
    src_row = (row_ids // ROWS) * ROWS + jnp.clip(row_ids % ROWS + row_shift, 0, ROWS - 1)
    src_col = (col_ids // COLS) * COLS + jnp.clip(col_ids % COLS + col_shift, 0, COLS - 1)
    flat_index = ((member * NY + src_row) * NX + src_col).astype(jnp.int32)
    picked = jnp.take(air_flux.reshape(-1), flat_index).astype(jnp.float32)
    return land_sea.astype(jnp.float32) * jnp.sum(remap_weight * picked, axis=0) / members


def reference(fields, diffusion, exchange_coef, sea_seen, remap_code, remap_weight, land_sea, fold_partner):
    members = N_COMP - 1
    states = []
    for member in range(N_COMP):
        current = fields[member]
        for substep in range(SUBSTEPS):
            current = diffuse(current, diffusion[member], fold_partner, member == members)
        states.append(current)
    sea_prior = sea_seen.astype(jnp.float32)
    fluxes = [(exchange_coef[member] * (sea_prior - states[member][0])).astype(jnp.bfloat16) for member in range(members)]
    air_flux = jnp.stack(fluxes)
    ocean_flux = remap(air_flux, remap_code, remap_weight, land_sea)
    updated = []
    surfaces = []
    for member in range(N_COMP):
        if member < members:
            surface = states[member][0] + air_gain * air_flux[member].astype(jnp.float32)
        else:
            surface = states[member][0] + ocean_flux
        surfaces.append(surface)
        updated.append(jnp.concatenate([surface[None], states[member][1:]], axis=0))
    sea_new = surfaces[members].astype(jnp.bfloat16).astype(jnp.float32)
    contrast = [sea_new - surfaces[member] for member in range(members)] + [sea_new - sea_prior]
    return jnp.stack(updated), jnp.stack(contrast)
```

```python
import functools

import jax
import jax.numpy as jnp
from jax import lax
from jax.experimental import pallas as pl
from jax.experimental.pallas import tpu as pltpu
from jax.sharding import PartitionSpec as P

MESH = pl.DeviceIdType.MESH
F32, BF16 = jnp.float32, jnp.bfloat16
ROWS, COLS, SLICES, TAPS, WIN = 48, 512, 8, 8, 4
PADR, PADC = 8, 128
EXTR, EXTC = ROWS + 2 * PADR, COLS + 2 * PADC
HALF = COLS // 2
BLOCKS = COLS // PADC
FOLD_ROWS = 24
N_SIDES = 8
AIR_GAIN = 0.5

MID_R, MID_C = pl.ds(PADR, ROWS), pl.ds(PADC, COLS)
LOW_R, HIGH_R = pl.ds(0, PADR), pl.ds(PADR + ROWS, PADR)
LOW_C, HIGH_C = pl.ds(0, PADC), pl.ds(PADC + COLS, PADC)
FIRST_R, LAST_R = pl.ds(PADR, PADR), pl.ds(ROWS, PADR)
FIRST_C, LAST_C = pl.ds(PADC, PADC), pl.ds(COLS, PADC)

SIDES = (
    (0, 1, LAST_R, MID_C, LOW_R, MID_C),
    (0, -1, FIRST_R, MID_C, HIGH_R, MID_C),
    (1, 0, MID_R, LAST_C, MID_R, LOW_C),
    (-1, 0, MID_R, FIRST_C, MID_R, HIGH_C),
    (1, 1, LAST_R, LAST_C, LOW_R, LOW_C),
    (-1, 1, LAST_R, FIRST_C, LOW_R, HIGH_C),
    (1, -1, FIRST_R, LAST_C, HIGH_R, LOW_C),
    (-1, -1, FIRST_R, FIRST_C, HIGH_R, HIGH_C),
)


def roll(value, shift, axis):
    return pltpu.roll(value, shift % value.shape[axis], axis)


def kernel(
    n_lon,
    n_lat,
    fields,
    diffusion,
    exchange,
    sea_seen,
    code,
    weight,
    land,
    fold,
    updated,
    contrast,
    ext,
    mid,
    upd,
    con,
    exch,
    seen,
    codes,
    weights,
    sea_mask,
    chosen,
    padded,
    shifted,
    share,
    share_in,
    part,
    part_in,
    surf,
    fold_out,
    fold_all,
    fold_at,
    load_sem,
    out_sem,
    halo_send,
    halo_recv,
    pair_send,
    pair_recv,
    fold_send,
    fold_recv,
    ready,
):
    lon, lat, comp = (lax.axis_index(a) for a in ("lon", "lat", "comp"))
    core = lax.rem(comp, 2)
    far = comp >= 2
    is_ocean = comp == 3
    folded = jnp.logical_and(is_ocean, lat == n_lat - 1)
    sibling = (lon, lat, comp + 1 - 2 * core)
    partner = (lon, lat, lax.rem(comp + 2, 4))

    def side_target(east, north):
        return (
            lax.rem(lon + east + n_lon, n_lon),
            lax.rem(lat + north + n_lat, n_lat),
            comp,
        )

    def has(north):
        if north == 0:
            return None
        return lat < n_lat - 1 if north > 0 else lat > 0

    def when(condition, action):
        if condition is None:
            action()
        else:
            pl.when(condition)(action)

    def local(src, dst, index):
        return pltpu.make_async_copy(src, dst, load_sem.at[index])

    loads = [
        local(diffusion.at[0], ext.at[0, MID_R, MID_C], 0),
        local(fields.at[0, 0], ext.at[1, MID_R, MID_C], 1),
        local(code, codes, 2),
        local(weight, weights, 3),
        local(sea_seen, seen, 4),
        local(exchange.at[0], exch, 5),
        local(land, sea_mask, 6),
        local(fields.at[0, pl.ds(1, SLICES - 1)], ext.at[pl.ds(2, SLICES - 1), MID_R, MID_C], 7),
    ]
    fold_load = local(fold.at[pl.ds(0, 1024)], fold_at, 8)
    for load in loads:
        load.start()

    barrier = pltpu.get_barrier_semaphore()

    def greet(target):
        pl.semaphore_signal(barrier, inc=1, device_id=target, device_id_type=MESH)

    for east, north, *_ in SIDES:
        when(has(north), functools.partial(greet, side_target(east, north)))
    greet(sibling)
    pl.when(jnp.logical_not(far))(functools.partial(greet, partner))

    @pl.when(folded)
    def _():
        fold_load.start()
        for away in range(1, n_lon):
            greet((lax.rem(lon + away, n_lon), lat, comp))

    @pl.when(lat == 0)
    def _():
        ext[:, 0:PADR, :] = jnp.zeros((SLICES + 1, PADR, EXTC), F32)

    @pl.when(lat == n_lat - 1)
    def _():
        ext[:, PADR + ROWS : EXTR, :] = jnp.zeros((SLICES + 1, PADR, EXTC), F32)

    expected = (
        3
        + 3 * (lat > 0).astype(jnp.int32)
        + 3 * (lat < n_lat - 1).astype(jnp.int32)
        + far.astype(jnp.int32)
        + (n_lon - 1) * folded.astype(jnp.int32)
    )
    pl.semaphore_wait(barrier, expected)

    @pl.when(far)
    def _():
        pl.semaphore_signal(ready, inc=1, device_id=partner, device_id_type=MESH)

    def halo(group, index):
        east, north, src_r, src_c, dst_r, dst_c = SIDES[index]
        if group == 1:
            planes = pl.ds(2, SLICES - 1)
        elif index < 4:
            planes = pl.ds(0, 2)
        else:
            planes = pl.ds(1, 1)
        slot = group * N_SIDES + index
        return pltpu.make_async_remote_copy(
            ext.at[planes, src_r, src_c],
            ext.at[planes, dst_r, dst_c],
            halo_send.at[slot],
            halo_recv.at[slot],
            device_id=side_target(east, north),
            device_id_type=MESH,
        )

    def send_halos(group):
        for index in range(N_SIDES):
            when(has(SIDES[index][1]), halo(group, index).start)

    def await_halos(group):
        for index in range(N_SIDES):
            when(has(-SIDES[index][1]), halo(group, index).wait_recv)

    def await_sent(group):
        for index in range(N_SIDES):
            when(has(SIDES[index][1]), halo(group, index).wait_send)

    loads[0].wait()
    loads[1].wait()
    send_halos(0)
    loads[7].wait()
    send_halos(1)

    def fold_copy(away):
        return pltpu.make_async_remote_copy(
            fold_out,
            fold_all.at[pl.ds(BLOCKS * lon, BLOCKS)],
            fold_send.at[away],
            fold_recv.at[away],
            device_id=(lax.rem(lon + away, n_lon), lat, comp),
            device_id_type=MESH,
        )

    @pl.when(folded)
    def _():
        fold_out[...] = jnp.zeros((BLOCKS, FOLD_ROWS, PADC), F32)
        for block in range(BLOCKS):
            at = PADC + block * PADC
            for plane in range(SLICES):
                tail = ext[plane + 1, ROWS : ROWS + PADR, at : at + PADC]
                fold_out[block, plane : plane + 1, :] = tail[6:7]
                fold_out[block, SLICES + plane : SLICES + plane + 1, :] = tail[7:8]
            tail = ext[0, ROWS : ROWS + PADR, at : at + PADC]
            fold_out[block, 2 * SLICES : 2 * SLICES + 1, :] = tail[7:8]
        fold_all[pl.ds(BLOCKS * lon, BLOCKS)] = fold_out[...]
        for away in range(1, n_lon):
            fold_copy(away).start()

    loads[2].wait()
    loads[3].wait()
    loads[4].wait()
    loads[5].wait()
    loads[6].wait()

    @pl.when(jnp.logical_not(is_ocean))
    def _():
        first = comp * (WIN * WIN)

        def rows_of(step, carry):
            at = pl.multiple_of(step * 8, 8)
            for block in range(BLOCKS):
                cols = slice(block * PADC, (block + 1) * PADC)
                tap_code = [codes[tap, pl.ds(at, 8), cols] - first for tap in range(TAPS)]
                tap_weight = [weights[tap, pl.ds(at, 8), cols] for tap in range(TAPS)]
                for cell in range(WIN * WIN):
                    terms = [jnp.where(c == cell, w, 0.0) for c, w in zip(tap_code, tap_weight)]
                    while len(terms) > 1:
                        terms = [a + b for a, b in zip(terms[::2], terms[1::2])]
                    chosen[cell, pl.ds(at, 8), cols] = terms[0]
            return carry

        lax.fori_loop(0, ROWS // 8, rows_of, 0)

    @pl.when(folded)
    def _():
        for away in range(1, n_lon):
            fold_copy(away).wait_recv()
        fold_load.wait()
        ahead = fold_at[0] + n_lon * COLS - (lon + 1) * COLS
        start = ahead // PADC
        rest = lax.rem(ahead, PADC)
        total = BLOCKS * n_lon
        window = [fold_all[lax.rem(start + i, total)] for i in range(BLOCKS + 2)]
        spots = lax.broadcasted_iota(jnp.int32, (2 * PADC, PADC), 0) + lax.broadcasted_iota(
            jnp.int32, (2 * PADC, PADC), 1
        )
        pick = jnp.where(spots == PADC + rest, 1.0, 0.0).astype(F32)
        for block in range(BLOCKS + 2):
            pair = jnp.concatenate([window[max(BLOCKS - block, 0)], window[BLOCKS + 1 - block]], axis=1)
            mirrored = jnp.dot(
                pair, pick, precision=lax.Precision.HIGHEST, preferred_element_type=F32
            )
            cols = slice(block * PADC, (block + 1) * PADC)
            beyond = PADR + ROWS
            for plane in range(SLICES):
                ext[plane + 1, beyond + 1 : beyond + 2, cols] = mirrored[plane : plane + 1]
                ext[plane + 1, beyond : beyond + 1, cols] = mirrored[
                    SLICES + plane : SLICES + plane + 1
                ]
            ext[0, beyond : beyond + 1, cols] = mirrored[2 * SLICES : 2 * SLICES + 1]

    def first_substep(plane):
        for block in range(EXTR // 8):
            at = block * 8
            here = ext[plane, at : at + 8, :]
            if block < EXTR // 8 - 1:
                north = ext[plane, at + 1 : at + 9, :]
            else:
                north = roll(here, -1, 0)
            if block > 0:
                south = ext[plane, at - 1 : at + 7, :]
            else:
                south = roll(here, 1, 0)
            east, west = roll(here, -1, 1), roll(here, 1, 1)
            rate = ext[0, at : at + 8, :]
            mid[plane - 1, at : at + 8, :] = here + rate * (north + south + east + west - 4.0 * here)

    def second_substep(plane, block):
        at = PADR + block * 8
        whole = mid[plane - 1, at : at + 8, :]
        here = whole[:, PADC : PADC + COLS]
        north = mid[plane - 1, at + 1 : at + 9, PADC : PADC + COLS]
        south = mid[plane - 1, at - 1 : at + 7, PADC : PADC + COLS]
        east = roll(whole, -1, 1)[:, PADC : PADC + COLS]
        west = roll(whole, 1, 1)[:, PADC : PADC + COLS]
        rate = ext[0, at : at + 8, PADC : PADC + COLS]
        return here + rate * (north + south + east + west - 4.0 * here)

    await_halos(0)
    first_substep(1)

    @pl.when(is_ocean)
    def _():
        for block in range(ROWS // 8):
            rows = slice(block * 8, block * 8 + 8)
            lowest = second_substep(1, block)
            share[0, rows, :] = lowest[:, :HALF]
            share[1, rows, :] = lowest[:, HALF:]

    @pl.when(jnp.logical_not(is_ocean))
    def _():
        for block in range(ROWS // 8):
            rows = slice(block * 8, block * 8 + 8)
            lowest = second_substep(1, block)
            flux = exch[rows, :] * (seen[rows, :].astype(F32) - lowest)
            flux = flux.astype(BF16).astype(F32)
            upd[0, rows, :] = lowest + AIR_GAIN * flux
            at = PADR + block * 8
            padded[at : at + 8, PADC : PADC + COLS] = flux
            padded[at : at + 8, :PADC] = jnp.broadcast_to(flux[:, :1], (8, PADC))
            padded[at : at + 8, PADC + COLS :] = jnp.broadcast_to(flux[:, COLS - 1 :], (8, PADC))
        padded[:PADR, :] = jnp.broadcast_to(padded[PADR : PADR + 1, :], (PADR, EXTC))
        end = PADR + ROWS
        padded[end:, :] = jnp.broadcast_to(padded[end - 1 : end, :], (PADR, EXTC))
        for block in range(EXTR // 8):
            at = block * 8
            whole = padded[at : at + 8, :]
            for step in range(WIN):
                shifted[step, at : at + 8, :] = roll(whole, 1 - step, 1)[:, PADC : PADC + COLS]
        for block in range(ROWS // 8):
            rows = slice(block * 8, block * 8 + 8)
            total = None
            for step in range(WIN):
                for up in range(WIN):
                    at = PADR + block * 8 + up - 1
                    term = chosen[WIN * up + step, rows, :] * shifted[step, at : at + 8, :]
                    total = term if total is None else total + term
            total = total * (sea_mask[rows, :].astype(F32) * (1.0 / 3.0))
            share[0, rows, :] = total[:, :HALF]
            share[1, rows, :] = total[:, HALF:]

    def pair_copy(index, src, dst, target):
        return pltpu.make_async_remote_copy(
            src, dst, pair_send.at[index], pair_recv.at[index], device_id=target, device_id_type=MESH
        )

    give = pair_copy(0, share.at[1 - core], share_in, sibling)
    cross = pair_copy(1, part, part_in, partner)
    finish = pair_copy(2, surf.at[core], surf.at[core], sibling)
    give.start()
    give.wait_recv()
    part[...] = share[core] + share_in[...]

    pl.when(far)(cross.start)

    await_halos(1)

    def other_slice(plane, carry):
        first_substep(plane)
        for block in range(ROWS // 8):
            upd[plane - 1, block * 8 : block * 8 + 8, :] = second_substep(plane, block)
        return carry

    lax.fori_loop(2, SLICES + 1, other_slice, 0)
    rest_out = pltpu.make_async_copy(
        upd.at[pl.ds(1, SLICES - 1)], updated.at[0, pl.ds(1, SLICES - 1)], out_sem.at[0]
    )
    top_out = pltpu.make_async_copy(upd.at[0], updated.at[0, 0], out_sem.at[1])
    con_out = pltpu.make_async_copy(con, contrast.at[0], out_sem.at[2])
    rest_out.start()

    @pl.when(jnp.logical_not(far))
    def _():
        pl.semaphore_wait(ready, 1)
        cross.start()

    pl.when(jnp.logical_not(is_ocean))(top_out.start)

    cross.wait_recv()
    surf[core] = part[...] + part_in[...]
    finish.start()
    finish.wait_recv()

    for block in range(ROWS // 8):
        rows = slice(block * 8, block * 8 + 8)
        ocean = jnp.concatenate([surf[0, rows, :], surf[1, rows, :]], axis=1)
        sea_new = ocean.astype(BF16).astype(F32)

        @pl.when(is_ocean)
        def _():
            upd[0, rows, :] = ocean
            con[rows, :] = sea_new - seen[rows, :].astype(F32)

        @pl.when(jnp.logical_not(is_ocean))
        def _():
            con[rows, :] = sea_new - upd[0, rows, :]

    con_out.start()
    pl.when(is_ocean)(top_out.start)

    await_sent(0)
    await_sent(1)
    give.wait_send()
    cross.wait_send()
    finish.wait_send()

    @pl.when(folded)
    def _():
        for away in range(1, n_lon):
            fold_copy(away).wait_send()

    rest_out.wait()
    top_out.wait()
    con_out.wait()


def shards(n_lon, n_lat, *args):
    fields = args[0]
    vmem, sems = pltpu.VMEM, pltpu.SemaphoreType.DMA
    return pl.pallas_call(
        functools.partial(kernel, n_lon, n_lat),
        out_shape=(
            jax.ShapeDtypeStruct(fields.shape, F32),
            jax.ShapeDtypeStruct((1, ROWS, COLS), F32),
        ),
        in_specs=[pl.BlockSpec(memory_space=pl.ANY)] * 8,
        out_specs=(pl.BlockSpec(memory_space=pl.ANY),) * 2,
        scratch_shapes=[
            vmem((SLICES + 1, EXTR, EXTC), F32),
            vmem((SLICES, EXTR, EXTC), F32),
            vmem((SLICES, ROWS, COLS), F32),
            vmem((ROWS, COLS), F32),
            vmem((ROWS, COLS), F32),
            vmem((ROWS, COLS), BF16),
            vmem((TAPS, ROWS, COLS), jnp.int32),
            vmem((TAPS, ROWS, COLS), F32),
            vmem((ROWS, COLS), jnp.int32),
            vmem((WIN * WIN, ROWS, COLS), F32),
            vmem((EXTR, EXTC), F32),
            vmem((WIN, EXTR, COLS), F32),
            vmem((2, ROWS, HALF), F32),
            vmem((ROWS, HALF), F32),
            vmem((ROWS, HALF), F32),
            vmem((ROWS, HALF), F32),
            vmem((2, ROWS, HALF), F32),
            vmem((BLOCKS, FOLD_ROWS, PADC), F32),
            vmem((BLOCKS * n_lon, FOLD_ROWS, PADC), F32),
            pltpu.SMEM((1024,), jnp.int32),
            sems((9,)),
            sems((3,)),
            sems((2 * N_SIDES,)),
            sems((2 * N_SIDES,)),
            sems((3,)),
            sems((3,)),
            sems((n_lon,)),
            sems((n_lon,)),
            pltpu.SemaphoreType.REGULAR,
        ],
        compiler_params=pltpu.CompilerParams(
            collective_id=0, has_side_effects=True, vmem_limit_bytes=32 * 2**20
        ),
    )(*args)


def solution(mesh):
    placed = (
        P("comp", None, "lat", "lon"),
        P("comp", "lat", "lon"),
        P("comp", "lat", "lon"),
        P("lat", "lon"),
        P(None, "lat", "lon"),
        P(None, "lat", "lon"),
        P("lat", "lon"),
        P(),
    )
    return jax.shard_map(
        functools.partial(shards, mesh.shape["lon"], mesh.shape["lat"]),
        mesh=mesh,
        in_specs=placed,
        out_specs=(P("comp", None, "lat", "lon"), P("comp", "lat", "lon")),
        check_vma=False,
    )
```

```python
import functools

import jax
import jax.numpy as jnp
from jax import lax
from jax.experimental import pallas as pl
from jax.experimental.pallas import tpu as pltpu
from jax.sharding import PartitionSpec as P

MESH = pl.DeviceIdType.MESH
F32, BF16 = jnp.float32, jnp.bfloat16
ROWS, COLS, SLICES, TAPS, WIN = 48, 512, 8, 8, 4
PADR, PADC = 8, 128
EXTR, EXTC = ROWS + 2 * PADR, COLS + 2 * PADC
HALF = COLS // 2
BLOCKS = COLS // PADC
N_SIDES = 8
AIR_GAIN = 0.5

MID_R, MID_C = pl.ds(PADR, ROWS), pl.ds(PADC, COLS)
LOW_R, HIGH_R = pl.ds(0, PADR), pl.ds(PADR + ROWS, PADR)
LOW_C, HIGH_C = pl.ds(0, PADC), pl.ds(PADC + COLS, PADC)
FIRST_R, LAST_R = pl.ds(PADR, PADR), pl.ds(ROWS, PADR)
FIRST_C, LAST_C = pl.ds(PADC, PADC), pl.ds(COLS, PADC)

SIDES = (
    (0, 1, LAST_R, MID_C, LOW_R, MID_C),
    (0, -1, FIRST_R, MID_C, HIGH_R, MID_C),
    (1, 0, MID_R, LAST_C, MID_R, LOW_C),
    (-1, 0, MID_R, FIRST_C, MID_R, HIGH_C),
    (1, 1, LAST_R, LAST_C, LOW_R, LOW_C),
    (-1, 1, LAST_R, FIRST_C, LOW_R, HIGH_C),
    (1, -1, FIRST_R, LAST_C, HIGH_R, LOW_C),
    (-1, -1, FIRST_R, FIRST_C, HIGH_R, HIGH_C),
)


FOLD_LINES = (
    ((1, 0, ROWS - 2), (1, 1, ROWS - 1), (0, 2, ROWS - 1)),
    tuple((plane, 8 * side + plane - 2, ROWS - 2 + side) for side in range(2) for plane in range(2, SLICES + 1)),
)


def roll(value, shift, axis):
    return pltpu.roll(value, shift % value.shape[axis], axis)


def kernel(
    n_lon,
    n_lat,
    fields,
    diffusion,
    exchange,
    sea_seen,
    code,
    weight,
    land,
    fold,
    updated,
    contrast,
    ext,
    mid,
    exch,
    seen,
    codes,
    weights,
    sea_mask,
    chosen,
    padded,
    shifted,
    share,
    share_in,
    part,
    part_in,
    surf,
    edge_out,
    side_out,
    rows_out,
    rows_in,
    corner_in,
    fold_out_0,
    fold_out_1,
    fold_all_0,
    fold_all_1,
    fold_at,
    load_sem,
    halo_send,
    halo_recv,
    pair_send,
    pair_recv,
    fold_send,
    fold_recv,
    ready,
):
    lon, lat, comp = (lax.axis_index(a) for a in ("lon", "lat", "comp"))
    core = lax.rem(comp, 2)
    far = comp >= 2
    is_ocean = comp == 3
    folded = jnp.logical_and(is_ocean, lat == n_lat - 1)
    fold_out, fold_all = (fold_out_0, fold_out_1), (fold_all_0, fold_all_1)
    sibling = (lon, lat, comp + 1 - 2 * core)
    partner = (lon, lat, lax.rem(comp + 2, 4))

    def side_target(east, north):
        return (
            lax.rem(lon + east + n_lon, n_lon),
            lax.rem(lat + north + n_lat, n_lat),
            comp,
        )

    def has(north):
        if north == 0:
            return None
        return lat < n_lat - 1 if north > 0 else lat > 0

    def when(condition, action):
        if condition is None:
            action()
        else:
            pl.when(condition)(action)

    def local(src, dst, index):
        return pltpu.make_async_copy(src, dst, load_sem.at[index])

    loads = [
        local(diffusion.at[0], ext.at[0, MID_R, MID_C], 0),
        local(fields.at[0, 0], ext.at[1, MID_R, MID_C], 1),
        local(code, codes, 2),
        local(weight, weights, 3),
        local(sea_seen, seen, 4),
        local(exchange.at[0], exch, 5),
        local(land, sea_mask, 6),
        local(fields.at[0, pl.ds(1, SLICES - 1)], ext.at[pl.ds(2, SLICES - 1), MID_R, MID_C], 7),
    ]
    fold_load = local(fold.at[pl.ds(0, 1024)], fold_at, 8)
    barrier = pltpu.get_barrier_semaphore()

    def greet(target):
        pl.semaphore_signal(barrier, inc=1, device_id=target, device_id_type=MESH)

    for east, north, *_ in SIDES:
        when(has(north), functools.partial(greet, side_target(east, north)))
    greet(sibling)
    pl.when(jnp.logical_not(far))(functools.partial(greet, partner))

    @pl.when(folded)
    def _():
        fold_load.start()
        for away in range(1, n_lon):
            greet((lax.rem(lon + away, n_lon), lat, comp))

    for load in loads:
        load.start()

    @pl.when(lat == 0)
    def _():
        ext[:, 0:PADR, :] = jnp.zeros((SLICES + 1, PADR, EXTC), F32)

    @pl.when(lat == n_lat - 1)
    def _():
        ext[:, PADR + ROWS : EXTR, :] = jnp.zeros((SLICES + 1, PADR, EXTC), F32)

    def halo(group, index):
        east, north, src_r, src_c, dst_r, dst_c = SIDES[index]
        way = 0 if north > 0 else 1
        if group == 1 and index < 2:
            src, dst = rows_out.at[way], rows_in.at[way]
        elif group == 1 and index >= 4:
            cells = pl.ds(COLS - PADC, PADC) if east > 0 else pl.ds(0, PADC)
            src, dst = rows_out.at[way, pl.ds(8 - 8 * way, 8), cells], corner_in.at[index - 4]
        elif group == 0 and index < 2:
            src, dst = edge_out.at[way], ext.at[1, dst_r, dst_c]
        elif group == 0 and index < 4:
            src, dst = side_out.at[index - 2], ext.at[1, dst_r, dst_c]
        else:
            planes = pl.ds(2, SLICES - 1) if group == 1 else pl.ds(1, 1)
            src, dst = ext.at[planes, src_r, src_c], ext.at[planes, dst_r, dst_c]
        slot = group * N_SIDES + index
        return pltpu.make_async_remote_copy(
            src,
            dst,
            halo_send.at[slot],
            halo_recv.at[slot],
            device_id=side_target(east, north),
            device_id_type=MESH,
        )

    def pack_surface():
        line = lax.broadcasted_iota(jnp.int32, (PADR, COLS), 0)
        for way, at, spare, turn in ((0, ROWS, 0, 1), (1, PADR, PADR - 1, -1)):
            tile = ext[1, at : at + PADR, PADC : PADC + COLS]
            rate = ext[0, at : at + PADR, PADC : PADC + COLS]
            edge_out[way] = jnp.where(line == spare, roll(rate, turn, 0), tile)
        lane = lax.broadcasted_iota(jnp.int32, (ROWS, PADC), 1)
        for way, at, spare, turn in ((0, COLS, 0, 1), (1, PADC, PADC - 1, -1)):
            tile = ext[1, PADR : PADR + ROWS, at : at + PADC]
            rate = ext[0, PADR : PADR + ROWS, at : at + PADC]
            side_out[way] = jnp.where(lane == spare, roll(rate, turn, 1), tile)

    def unpack_surface():
        @pl.when(lat > 0)
        def _():
            ext[0, :PADR, PADC : PADC + COLS] = roll(ext[1, :PADR, PADC : PADC + COLS], -1, 0)

        @pl.when(lat < n_lat - 1)
        def _():
            beyond = slice(PADR + ROWS, EXTR)
            ext[0, beyond, PADC : PADC + COLS] = roll(ext[1, beyond, PADC : PADC + COLS], 1, 0)

        rows = slice(PADR, PADR + ROWS)
        ext[0, rows, :PADC] = roll(ext[1, rows, :PADC], -1, 1)
        ext[0, rows, PADC + COLS :] = roll(ext[1, rows, PADC + COLS :], 1, 1)

    def pack_rows():
        for plane in range(2, SLICES + 1):
            at = plane - 2
            tail = ext[plane, ROWS : ROWS + PADR, PADC : PADC + COLS]
            head = ext[plane, PADR : 2 * PADR, PADC : PADC + COLS]
            rows_out[0, at : at + 1, :] = tail[6:7]
            rows_out[0, 8 + at : 9 + at, :] = tail[7:8]
            rows_out[1, at : at + 1, :] = head[0:1]
            rows_out[1, 8 + at : 9 + at, :] = head[1:2]
        for way in range(2):
            for at in (7, 15):
                rows_out[way, at : at + 1, :] = jnp.zeros((1, COLS), F32)

    def unpack_rows():
        beyond = PADR + ROWS
        sides = (slice(0, PADC), slice(PADC + COLS, EXTC))

        @pl.when(lat > 0)
        def _():
            for plane in range(2, SLICES + 1):
                at = plane - 2
                ext[plane, PADR - 2 : PADR - 1, PADC : PADC + COLS] = rows_in[0, at : at + 1, :]
                ext[plane, PADR - 1 : PADR, PADC : PADC + COLS] = rows_in[0, 8 + at : 9 + at, :]
                for side in range(2):
                    ext[plane, PADR - 1 : PADR, sides[side]] = corner_in[side, at : at + 1, :]

        @pl.when(lat < n_lat - 1)
        def _():
            for plane in range(2, SLICES + 1):
                at = plane - 2
                ext[plane, beyond : beyond + 1, PADC : PADC + COLS] = rows_in[1, at : at + 1, :]
                ext[plane, beyond + 1 : beyond + 2, PADC : PADC + COLS] = rows_in[1, 8 + at : 9 + at, :]
                for side in range(2):
                    ext[plane, beyond : beyond + 1, sides[side]] = corner_in[2 + side, at : at + 1, :]

    def send_halos(group):
        for index in reversed(range(N_SIDES)):
            when(has(SIDES[index][1]), halo(group, index).start)

    def await_halos(group):
        for index in range(N_SIDES):
            when(has(-SIDES[index][1]), halo(group, index).wait_recv)

    def await_sent(group):
        for index in range(N_SIDES):
            when(has(SIDES[index][1]), halo(group, index).wait_send)

    loads[0].wait()
    loads[1].wait()
    pack_surface()
    expected = (
        3
        + 3 * (lat > 0).astype(jnp.int32)
        + 3 * (lat < n_lat - 1).astype(jnp.int32)
        + far.astype(jnp.int32)
        + (n_lon - 1) * folded.astype(jnp.int32)
    )
    pl.semaphore_wait(barrier, expected)

    @pl.when(far)
    def _():
        pl.semaphore_signal(ready, inc=1, device_id=partner, device_id_type=MESH)

    send_halos(0)

    def fold_copy(group, away):
        return pltpu.make_async_remote_copy(
            fold_out[group],
            fold_all[group].at[pl.ds(BLOCKS * lon, BLOCKS)],
            fold_send.at[group, away],
            fold_recv.at[group, away],
            device_id=(lax.rem(lon + away, n_lon), lat, comp),
            device_id_type=MESH,
        )

    def fold_pack(group):
        for block in range(BLOCKS):
            cols = slice(PADC + block * PADC, 2 * PADC + block * PADC)
            for plane, at, row in FOLD_LINES[group]:
                fold_out[group][block, at : at + 1, :] = ext[plane, PADR + row : PADR + row + 1, cols]
        fold_all[group][pl.ds(BLOCKS * lon, BLOCKS)] = fold_out[group][...]
        for away in range(1, n_lon):
            fold_copy(group, away).start()

    def fold_unpack(group):
        for away in range(1, n_lon):
            fold_copy(group, away).wait_recv()
        ahead = fold_at[0] + n_lon * COLS - (lon + 1) * COLS
        start = ahead // PADC
        rest = lax.rem(ahead, PADC)
        window = [fold_all[group][lax.rem(start + i, BLOCKS * n_lon)] for i in range(BLOCKS + 2)]
        spots = lax.broadcasted_iota(jnp.int32, (2 * PADC, PADC), 0) + lax.broadcasted_iota(
            jnp.int32, (2 * PADC, PADC), 1
        )
        pick = jnp.where(spots == PADC + rest, 1.0, 0.0).astype(F32)
        for block in range(BLOCKS + 2):
            pair = jnp.concatenate([window[max(BLOCKS - block, 0)], window[BLOCKS + 1 - block]], axis=1)
            mirrored = jnp.dot(
                pair, pick, precision=lax.Precision.HIGHEST, preferred_element_type=F32
            )
            cols = slice(block * PADC, (block + 1) * PADC)
            for plane, at, row in FOLD_LINES[group]:
                to = PADR + 2 * ROWS - 1 - row
                ext[plane, to : to + 1, cols] = mirrored[at : at + 1]

    @pl.when(folded)
    def _():
        for packed in fold_out:
            packed[...] = jnp.zeros(packed.shape, F32)
        fold_pack(0)

    loads[7].wait()
    pack_rows()
    send_halos(1)

    @pl.when(folded)
    def _():
        fold_pack(1)

    loads[2].wait()
    loads[3].wait()
    loads[4].wait()
    loads[5].wait()
    loads[6].wait()

    @pl.when(jnp.logical_not(is_ocean))
    def _():
        first = comp * (WIN * WIN)

        def rows_of(step, carry):
            at = pl.multiple_of(step * 8, 8)
            for block in range(BLOCKS):
                cols = slice(block * PADC, (block + 1) * PADC)
                tap_code = [codes[tap, pl.ds(at, 8), cols] - first for tap in range(TAPS)]
                tap_weight = [weights[tap, pl.ds(at, 8), cols] for tap in range(TAPS)]
                for cell in range(WIN * WIN):
                    terms = [jnp.where(c == cell, w, 0.0) for c, w in zip(tap_code, tap_weight)]
                    while len(terms) > 1:
                        terms = [a + b for a, b in zip(terms[::2], terms[1::2])]
                    chosen[cell, pl.ds(at, 8), cols] = terms[0]
            return carry

        lax.fori_loop(0, ROWS // 8, rows_of, 0)

    def first_substep(plane):
        for block in range(EXTR // 8):
            at = block * 8
            here = ext[plane, at : at + 8, :]
            if block < EXTR // 8 - 1:
                north = ext[plane, at + 1 : at + 9, :]
            else:
                north = roll(here, -1, 0)
            if block > 0:
                south = ext[plane, at - 1 : at + 7, :]
            else:
                south = roll(here, 1, 0)
            east, west = roll(here, -1, 1), roll(here, 1, 1)
            rate = ext[0, at : at + 8, :]
            mid[plane - 1, at : at + 8, :] = here + rate * (north + south + east + west - 4.0 * here)

    def second_substep(plane, block):
        at = PADR + block * 8
        whole = mid[plane - 1, at : at + 8, :]
        here = whole[:, PADC : PADC + COLS]
        north = mid[plane - 1, at + 1 : at + 9, PADC : PADC + COLS]
        south = mid[plane - 1, at - 1 : at + 7, PADC : PADC + COLS]
        east = roll(whole, -1, 1)[:, PADC : PADC + COLS]
        west = roll(whole, 1, 1)[:, PADC : PADC + COLS]
        rate = ext[0, at : at + 8, PADC : PADC + COLS]
        return here + rate * (north + south + east + west - 4.0 * here)

    await_halos(0)
    unpack_surface()

    @pl.when(folded)
    def _():
        fold_load.wait()
        fold_unpack(0)

    first_substep(1)

    @pl.when(is_ocean)
    def _():
        for block in range(ROWS // 8):
            rows = slice(block * 8, block * 8 + 8)
            lowest = second_substep(1, block)
            share[0, rows, :] = lowest[:, :HALF]
            share[1, rows, :] = lowest[:, HALF:]

    @pl.when(jnp.logical_not(is_ocean))
    def _():
        for block in range(ROWS // 8):
            rows = slice(block * 8, block * 8 + 8)
            lowest = second_substep(1, block)
            flux = exch[rows, :] * (seen[rows, :].astype(F32) - lowest)
            flux = flux.astype(BF16).astype(F32)
            updated[0, 0, rows, :] = lowest + AIR_GAIN * flux
            at = PADR + block * 8
            padded[at : at + 8, PADC : PADC + COLS] = flux
            padded[at : at + 8, :PADC] = jnp.broadcast_to(flux[:, :1], (8, PADC))
            padded[at : at + 8, PADC + COLS :] = jnp.broadcast_to(flux[:, COLS - 1 :], (8, PADC))
        padded[:PADR, :] = jnp.broadcast_to(padded[PADR : PADR + 1, :], (PADR, EXTC))
        end = PADR + ROWS
        padded[end:, :] = jnp.broadcast_to(padded[end - 1 : end, :], (PADR, EXTC))
        for block in range(EXTR // 8):
            at = block * 8
            whole = padded[at : at + 8, :]
            for step in range(WIN):
                shifted[step, at : at + 8, :] = roll(whole, 1 - step, 1)[:, PADC : PADC + COLS]
        for block in range(ROWS // 8):
            rows = slice(block * 8, block * 8 + 8)
            total = None
            for step in range(WIN):
                for up in range(WIN):
                    at = PADR + block * 8 + up - 1
                    term = chosen[WIN * up + step, rows, :] * shifted[step, at : at + 8, :]
                    total = term if total is None else total + term
            total = total * (sea_mask[rows, :].astype(F32) * (1.0 / 3.0))
            share[0, rows, :] = total[:, :HALF]
            share[1, rows, :] = total[:, HALF:]

    def pair_copy(index, src, dst, target):
        return pltpu.make_async_remote_copy(
            src, dst, pair_send.at[index], pair_recv.at[index], device_id=target, device_id_type=MESH
        )

    give = pair_copy(0, share.at[1 - core], share_in, sibling)
    cross = pair_copy(1, part, part_in, partner)
    finish = pair_copy(2, surf.at[core], surf.at[core], sibling)
    give.start()
    give.wait_recv()
    part[...] = share[core] + share_in[...]

    pl.when(far)(cross.start)

    await_halos(1)
    unpack_rows()

    @pl.when(folded)
    def _():
        fold_unpack(1)

    def other_slice(plane, carry):
        first_substep(plane)
        for block in range(ROWS // 8):
            updated[0, plane - 1, block * 8 : block * 8 + 8, :] = second_substep(plane, block)
        return carry

    lax.fori_loop(2, SLICES + 1, other_slice, 0)

    @pl.when(jnp.logical_not(far))
    def _():
        pl.semaphore_wait(ready, 1)
        cross.start()

    cross.wait_recv()
    surf[core] = part[...] + part_in[...]
    finish.start()

    finish.wait_recv()

    for block in range(ROWS // 8):
        rows = slice(block * 8, block * 8 + 8)
        ocean = jnp.concatenate([surf[0, rows, :], surf[1, rows, :]], axis=1)
        sea_new = ocean.astype(BF16).astype(F32)

        @pl.when(is_ocean)
        def _():
            updated[0, 0, rows, :] = ocean
            contrast[0, rows, :] = sea_new - seen[rows, :].astype(F32)

        @pl.when(jnp.logical_not(is_ocean))
        def _():
            contrast[0, rows, :] = sea_new - updated[0, 0, rows, :]

    await_sent(0)
    await_sent(1)
    give.wait_send()
    cross.wait_send()
    finish.wait_send()

    @pl.when(folded)
    def _():
        for away in range(1, n_lon):
            fold_copy(0, away).wait_send()
            fold_copy(1, away).wait_send()


def shards(n_lon, n_lat, *args):
    fields = args[0]
    vmem, sems = pltpu.VMEM, pltpu.SemaphoreType.DMA
    return pl.pallas_call(
        functools.partial(kernel, n_lon, n_lat),
        out_shape=(
            pltpu.VMEM(fields.shape, F32),
            pltpu.VMEM((1, ROWS, COLS), F32),
        ),
        in_specs=[pl.BlockSpec(memory_space=pl.ANY)] * 8,
        out_specs=(pl.BlockSpec(memory_space=pltpu.VMEM),) * 2,
        scratch_shapes=[
            vmem((SLICES + 1, EXTR, EXTC), F32),
            vmem((SLICES, EXTR, EXTC), F32),
            vmem((ROWS, COLS), F32),
            vmem((ROWS, COLS), BF16),
            vmem((TAPS, ROWS, COLS), jnp.int32),
            vmem((TAPS, ROWS, COLS), F32),
            vmem((ROWS, COLS), jnp.int32),
            vmem((WIN * WIN, ROWS, COLS), F32),
            vmem((EXTR, EXTC), F32),
            vmem((WIN, EXTR, COLS), F32),
            vmem((2, ROWS, HALF), F32),
            vmem((ROWS, HALF), F32),
            vmem((ROWS, HALF), F32),
            vmem((ROWS, HALF), F32),
            vmem((2, ROWS, HALF), F32),
            vmem((2, PADR, COLS), F32),
            vmem((2, ROWS, PADC), F32),
            vmem((2, 16, COLS), F32),
            vmem((2, 16, COLS), F32),
            vmem((4, 8, PADC), F32),
            vmem((BLOCKS, 8, PADC), F32),
            vmem((BLOCKS, 16, PADC), F32),
            vmem((BLOCKS * n_lon, 8, PADC), F32),
            vmem((BLOCKS * n_lon, 16, PADC), F32),
            pltpu.SMEM((1024,), jnp.int32),
            sems((9,)),
            sems((2 * N_SIDES,)),
            sems((2 * N_SIDES,)),
            sems((3,)),
            sems((3,)),
            sems((2, n_lon)),
            sems((2, n_lon)),
            pltpu.SemaphoreType.REGULAR,
        ],
        compiler_params=pltpu.CompilerParams(
            collective_id=0, has_side_effects=True, vmem_limit_bytes=32 * 2**20
        ),
    )(*[pltpu.with_memory_space_constraint(a, pltpu.HBM) for a in args])


def solution(mesh):
    placed = (
        P("comp", None, "lat", "lon"),
        P("comp", "lat", "lon"),
        P("comp", "lat", "lon"),
        P("lat", "lon"),
        P(None, "lat", "lon"),
        P(None, "lat", "lon"),
        P("lat", "lon"),
        P(),
    )
    return jax.shard_map(
        functools.partial(shards, mesh.shape["lon"], mesh.shape["lat"]),
        mesh=mesh,
        in_specs=placed,
        out_specs=(P("comp", None, "lat", "lon"), P("comp", "lat", "lon")),
        check_vma=False,
    )
```

```python
import functools

import jax
import jax.numpy as jnp
from jax import lax
from jax.experimental import pallas as pl
from jax.experimental.pallas import tpu as pltpu
from jax.sharding import PartitionSpec as P

MESH = pl.DeviceIdType.MESH
F32, BF16 = jnp.float32, jnp.bfloat16
ROWS, COLS, SLICES, TAPS, WIN = 48, 512, 8, 8, 4
PADR, PADC = 8, 128
EXTR, EXTC = ROWS + 2 * PADR, COLS + 2 * PADC
HALF = COLS // 2
BLOCKS = COLS // PADC
N_SIDES = 8
AIR_GAIN = 0.5

MID_R, MID_C = pl.ds(PADR, ROWS), pl.ds(PADC, COLS)
LOW_R, HIGH_R = pl.ds(0, PADR), pl.ds(PADR + ROWS, PADR)
LOW_C, HIGH_C = pl.ds(0, PADC), pl.ds(PADC + COLS, PADC)
FIRST_R, LAST_R = pl.ds(PADR, PADR), pl.ds(ROWS, PADR)
FIRST_C, LAST_C = pl.ds(PADC, PADC), pl.ds(COLS, PADC)

SIDES = (
    (0, 1, LAST_R, MID_C, LOW_R, MID_C),
    (0, -1, FIRST_R, MID_C, HIGH_R, MID_C),
    (1, 0, MID_R, LAST_C, MID_R, LOW_C),
    (-1, 0, MID_R, FIRST_C, MID_R, HIGH_C),
    (1, 1, LAST_R, LAST_C, LOW_R, LOW_C),
    (-1, 1, LAST_R, FIRST_C, LOW_R, HIGH_C),
    (1, -1, FIRST_R, LAST_C, HIGH_R, LOW_C),
    (-1, -1, FIRST_R, FIRST_C, HIGH_R, HIGH_C),
)


FOLD_LINES = (
    ((1, 0, ROWS - 2), (1, 1, ROWS - 1), (0, 2, ROWS - 1)),
    tuple((plane, 8 * side + plane - 2, ROWS - 2 + side) for side in range(2) for plane in range(2, SLICES + 1)),
)


def roll(value, shift, axis):
    return pltpu.roll(value, shift % value.shape[axis], axis)


def kernel(
    n_lon,
    n_lat,
    fields,
    diffusion,
    exchange,
    sea_seen,
    code,
    weight,
    land,
    fold,
    updated,
    contrast,
    ext,
    mid,
    exch,
    seen,
    codes,
    weights,
    sea_mask,
    chosen,
    padded,
    shifted,
    share,
    share_in,
    part,
    part_in,
    surf,
    edge_out,
    side_out,
    rows_out,
    rows_in,
    corner_in,
    fold_out_0,
    fold_out_1,
    fold_all_0,
    fold_all_1,
    fold_at,
    load_sem,
    halo_send,
    halo_recv,
    pair_send,
    pair_recv,
    fold_send,
    fold_recv,
    ready,
):
    lon, lat, comp = (lax.axis_index(a) for a in ("lon", "lat", "comp"))
    core = lax.rem(comp, 2)
    far = comp >= 2
    is_ocean = comp == 3
    folded = jnp.logical_and(is_ocean, lat == n_lat - 1)
    fold_out, fold_all = (fold_out_0, fold_out_1), (fold_all_0, fold_all_1)
    sibling = (lon, lat, comp + 1 - 2 * core)
    partner = (lon, lat, lax.rem(comp + 2, 4))

    def side_target(east, north):
        return (
            lax.rem(lon + east + n_lon, n_lon),
            lax.rem(lat + north + n_lat, n_lat),
            comp,
        )

    def has(north):
        if north == 0:
            return None
        return lat < n_lat - 1 if north > 0 else lat > 0

    def when(condition, action):
        if condition is None:
            action()
        else:
            pl.when(condition)(action)

    def local(src, dst, index):
        return pltpu.make_async_copy(src, dst, load_sem.at[index])

    loads = [
        local(diffusion.at[0], ext.at[0, MID_R, MID_C], 0),
        local(fields.at[0, 0], ext.at[1, MID_R, MID_C], 1),
        local(code, codes, 2),
        local(weight, weights, 3),
        local(sea_seen, seen, 4),
        local(exchange.at[0], exch, 5),
        local(land, sea_mask, 6),
        local(fields.at[0, pl.ds(1, SLICES - 1)], ext.at[pl.ds(2, SLICES - 1), MID_R, MID_C], 7),
    ]
    fold_load = local(fold.at[pl.ds(0, 1024)], fold_at, 8)
    barrier = pltpu.get_barrier_semaphore()

    def greet(target):
        pl.semaphore_signal(barrier, inc=1, device_id=target, device_id_type=MESH)

    for east, north, *_ in SIDES:
        when(has(north), functools.partial(greet, side_target(east, north)))
    greet(sibling)
    pl.when(jnp.logical_not(far))(functools.partial(greet, partner))

    @pl.when(folded)
    def _():
        fold_load.start()
        for away in range(1, n_lon):
            greet((lax.rem(lon + away, n_lon), lat, comp))

    for load in loads:
        load.start()

    @pl.when(lat == 0)
    def _():
        ext[:, 0:PADR, :] = jnp.zeros((SLICES + 1, PADR, EXTC), F32)

    @pl.when(lat == n_lat - 1)
    def _():
        ext[:, PADR + ROWS : EXTR, :] = jnp.zeros((SLICES + 1, PADR, EXTC), F32)

    def halo(group, index):
        east, north, src_r, src_c, dst_r, dst_c = SIDES[index]
        way = 0 if north > 0 else 1
        if group == 1 and index < 2:
            src, dst = rows_out.at[way], rows_in.at[way]
        elif group == 1 and index >= 4:
            cells = pl.ds(COLS - PADC, PADC) if east > 0 else pl.ds(0, PADC)
            src, dst = rows_out.at[way, pl.ds(8 - 8 * way, 8), cells], corner_in.at[index - 4]
        elif group == 0 and index < 2:
            src, dst = edge_out.at[way], ext.at[1, dst_r, dst_c]
        elif group == 0 and index < 4:
            src, dst = side_out.at[index - 2], ext.at[1, dst_r, dst_c]
        else:
            planes = pl.ds(2, SLICES - 1) if group == 1 else pl.ds(1, 1)
            src, dst = ext.at[planes, src_r, src_c], ext.at[planes, dst_r, dst_c]
        slot = group * N_SIDES + index
        return pltpu.make_async_remote_copy(
            src,
            dst,
            halo_send.at[slot],
            halo_recv.at[slot],
            device_id=side_target(east, north),
            device_id_type=MESH,
        )

    def pack_surface():
        line = lax.broadcasted_iota(jnp.int32, (PADR, COLS), 0)
        for way, at, spare, turn in ((0, ROWS, 0, 1), (1, PADR, PADR - 1, -1)):
            tile = ext[1, at : at + PADR, PADC : PADC + COLS]
            rate = ext[0, at : at + PADR, PADC : PADC + COLS]
            edge_out[way] = jnp.where(line == spare, roll(rate, turn, 0), tile)
        lane = lax.broadcasted_iota(jnp.int32, (ROWS, PADC), 1)
        for way, at, spare, turn in ((0, COLS, 0, 1), (1, PADC, PADC - 1, -1)):
            tile = ext[1, PADR : PADR + ROWS, at : at + PADC]
            rate = ext[0, PADR : PADR + ROWS, at : at + PADC]
            side_out[way] = jnp.where(lane == spare, roll(rate, turn, 1), tile)

    def unpack_surface():
        @pl.when(lat > 0)
        def _():
            ext[0, :PADR, PADC : PADC + COLS] = roll(ext[1, :PADR, PADC : PADC + COLS], -1, 0)

        @pl.when(lat < n_lat - 1)
        def _():
            beyond = slice(PADR + ROWS, EXTR)
            ext[0, beyond, PADC : PADC + COLS] = roll(ext[1, beyond, PADC : PADC + COLS], 1, 0)

        rows = slice(PADR, PADR + ROWS)
        ext[0, rows, :PADC] = roll(ext[1, rows, :PADC], -1, 1)
        ext[0, rows, PADC + COLS :] = roll(ext[1, rows, PADC + COLS :], 1, 1)

    def pack_rows():
        for plane in range(2, SLICES + 1):
            at = plane - 2
            tail = ext[plane, ROWS : ROWS + PADR, PADC : PADC + COLS]
            head = ext[plane, PADR : 2 * PADR, PADC : PADC + COLS]
            rows_out[0, at : at + 1, :] = tail[6:7]
            rows_out[0, 8 + at : 9 + at, :] = tail[7:8]
            rows_out[1, at : at + 1, :] = head[0:1]
            rows_out[1, 8 + at : 9 + at, :] = head[1:2]
        for way in range(2):
            for at in (7, 15):
                rows_out[way, at : at + 1, :] = jnp.zeros((1, COLS), F32)

    def unpack_rows():
        beyond = PADR + ROWS
        sides = (slice(0, PADC), slice(PADC + COLS, EXTC))

        @pl.when(lat > 0)
        def _():
            for plane in range(2, SLICES + 1):
                at = plane - 2
                ext[plane, PADR - 2 : PADR - 1, PADC : PADC + COLS] = rows_in[0, at : at + 1, :]
                ext[plane, PADR - 1 : PADR, PADC : PADC + COLS] = rows_in[0, 8 + at : 9 + at, :]
                for side in range(2):
                    ext[plane, PADR - 1 : PADR, sides[side]] = corner_in[side, at : at + 1, :]

        @pl.when(lat < n_lat - 1)
        def _():
            for plane in range(2, SLICES + 1):
                at = plane - 2
                ext[plane, beyond : beyond + 1, PADC : PADC + COLS] = rows_in[1, at : at + 1, :]
                ext[plane, beyond + 1 : beyond + 2, PADC : PADC + COLS] = rows_in[1, 8 + at : 9 + at, :]
                for side in range(2):
                    ext[plane, beyond : beyond + 1, sides[side]] = corner_in[2 + side, at : at + 1, :]

    def send_halos(group):
        for index in reversed(range(N_SIDES)):
            when(has(SIDES[index][1]), halo(group, index).start)

    def await_halos(group):
        for index in range(N_SIDES):
            when(has(-SIDES[index][1]), halo(group, index).wait_recv)

    def await_sent(group):
        for index in range(N_SIDES):
            when(has(SIDES[index][1]), halo(group, index).wait_send)

    loads[0].wait()
    loads[1].wait()
    pack_surface()
    expected = (
        3
        + 3 * (lat > 0).astype(jnp.int32)
        + 3 * (lat < n_lat - 1).astype(jnp.int32)
        + far.astype(jnp.int32)
        + (n_lon - 1) * folded.astype(jnp.int32)
    )
    pl.semaphore_wait(barrier, expected)

    @pl.when(far)
    def _():
        pl.semaphore_signal(ready, inc=1, device_id=partner, device_id_type=MESH)

    send_halos(0)

    def fold_copy(group, away):
        return pltpu.make_async_remote_copy(
            fold_out[group],
            fold_all[group].at[pl.ds(BLOCKS * lon, BLOCKS)],
            fold_send.at[group, away],
            fold_recv.at[group, away],
            device_id=(lax.rem(lon + away, n_lon), lat, comp),
            device_id_type=MESH,
        )

    def fold_pack(group):
        for block in range(BLOCKS):
            cols = slice(PADC + block * PADC, 2 * PADC + block * PADC)
            for plane, at, row in FOLD_LINES[group]:
                fold_out[group][block, at : at + 1, :] = ext[plane, PADR + row : PADR + row + 1, cols]
        fold_all[group][pl.ds(BLOCKS * lon, BLOCKS)] = fold_out[group][...]
        for away in range(1, n_lon):
            fold_copy(group, away).start()

    def fold_unpack(group):
        for away in range(1, n_lon):
            fold_copy(group, away).wait_recv()
        ahead = fold_at[0] + n_lon * COLS - (lon + 1) * COLS
        start = ahead // PADC
        rest = lax.rem(ahead, PADC)
        window = [fold_all[group][lax.rem(start + i, BLOCKS * n_lon)] for i in range(BLOCKS + 2)]
        spots = lax.broadcasted_iota(jnp.int32, (2 * PADC, PADC), 0) + lax.broadcasted_iota(
            jnp.int32, (2 * PADC, PADC), 1
        )
        pick = jnp.where(spots == PADC + rest, 1.0, 0.0).astype(F32)
        for block in range(BLOCKS + 2):
            pair = jnp.concatenate([window[max(BLOCKS - block, 0)], window[BLOCKS + 1 - block]], axis=1)
            mirrored = jnp.dot(
                pair, pick, precision=lax.Precision.HIGHEST, preferred_element_type=F32
            )
            cols = slice(block * PADC, (block + 1) * PADC)
            for plane, at, row in FOLD_LINES[group]:
                to = PADR + 2 * ROWS - 1 - row
                ext[plane, to : to + 1, cols] = mirrored[at : at + 1]

    @pl.when(folded)
    def _():
        for packed in fold_out:
            packed[...] = jnp.zeros(packed.shape, F32)
        fold_pack(0)

    loads[7].wait()
    pack_rows()
    send_halos(1)

    @pl.when(folded)
    def _():
        fold_pack(1)

    loads[2].wait()
    loads[3].wait()
    loads[4].wait()
    loads[5].wait()
    loads[6].wait()

    @pl.when(jnp.logical_not(is_ocean))
    def _():
        first = comp * (WIN * WIN)

        def rows_of(step, carry):
            at = pl.multiple_of(step * 8, 8)
            for block in range(BLOCKS):
                cols = slice(block * PADC, (block + 1) * PADC)
                tap_code = [codes[tap, pl.ds(at, 8), cols] - first for tap in range(TAPS)]
                tap_weight = [weights[tap, pl.ds(at, 8), cols] for tap in range(TAPS)]
                for cell in range(WIN * WIN):
                    terms = [jnp.where(c == cell, w, 0.0) for c, w in zip(tap_code, tap_weight)]
                    while len(terms) > 1:
                        terms = [a + b for a, b in zip(terms[::2], terms[1::2])]
                    chosen[cell, pl.ds(at, 8), cols] = terms[0]
            return carry

        lax.fori_loop(0, ROWS // 8, rows_of, 0)

    def first_substep(plane):
        for block in range(EXTR // 8):
            at = block * 8
            here = ext[plane, at : at + 8, :]
            if block < EXTR // 8 - 1:
                north = ext[plane, at + 1 : at + 9, :]
            else:
                north = roll(here, -1, 0)
            if block > 0:
                south = ext[plane, at - 1 : at + 7, :]
            else:
                south = roll(here, 1, 0)
            east, west = roll(here, -1, 1), roll(here, 1, 1)
            rate = ext[0, at : at + 8, :]
            mid[plane - 1, at : at + 8, :] = here + rate * (north + south + east + west - 4.0 * here)

    def second_substep(plane, block):
        at = PADR + block * 8
        whole = mid[plane - 1, at : at + 8, :]
        here = whole[:, PADC : PADC + COLS]
        north = mid[plane - 1, at + 1 : at + 9, PADC : PADC + COLS]
        south = mid[plane - 1, at - 1 : at + 7, PADC : PADC + COLS]
        east = roll(whole, -1, 1)[:, PADC : PADC + COLS]
        west = roll(whole, 1, 1)[:, PADC : PADC + COLS]
        rate = ext[0, at : at + 8, PADC : PADC + COLS]
        return here + rate * (north + south + east + west - 4.0 * here)

    await_halos(0)
    unpack_surface()

    @pl.when(folded)
    def _():
        fold_load.wait()
        fold_unpack(0)

    first_substep(1)

    @pl.when(is_ocean)
    def _():
        for block in range(ROWS // 8):
            rows = slice(block * 8, block * 8 + 8)
            lowest = second_substep(1, block)
            share[0, rows, :] = lowest[:, :HALF]
            share[1, rows, :] = lowest[:, HALF:]

    @pl.when(jnp.logical_not(is_ocean))
    def _():
        for block in range(ROWS // 8):
            rows = slice(block * 8, block * 8 + 8)
            lowest = second_substep(1, block)
            flux = exch[rows, :] * (seen[rows, :].astype(F32) - lowest)
            flux = flux.astype(BF16).astype(F32)
            updated[0, 0, rows, :] = lowest + AIR_GAIN * flux
            at = PADR + block * 8
            padded[at : at + 8, PADC : PADC + COLS] = flux
            padded[at : at + 8, :PADC] = jnp.broadcast_to(flux[:, :1], (8, PADC))
            padded[at : at + 8, PADC + COLS :] = jnp.broadcast_to(flux[:, COLS - 1 :], (8, PADC))
        padded[:PADR, :] = jnp.broadcast_to(padded[PADR : PADR + 1, :], (PADR, EXTC))
        end = PADR + ROWS
        padded[end:, :] = jnp.broadcast_to(padded[end - 1 : end, :], (PADR, EXTC))
        for block in range(EXTR // 8):
            at = block * 8
            whole = padded[at : at + 8, :]
            for step in range(WIN):
                shifted[step, at : at + 8, :] = roll(whole, 1 - step, 1)[:, PADC : PADC + COLS]
        for block in range(ROWS // 8):
            rows = slice(block * 8, block * 8 + 8)
            total = None
            for step in range(WIN):
                for up in range(WIN):
                    at = PADR + block * 8 + up - 1
                    term = chosen[WIN * up + step, rows, :] * shifted[step, at : at + 8, :]
                    total = term if total is None else total + term
            total = total * (sea_mask[rows, :].astype(F32) * (1.0 / 3.0))
            share[0, rows, :] = total[:, :HALF]
            share[1, rows, :] = total[:, HALF:]

    def pair_copy(index, src, dst, target):
        return pltpu.make_async_remote_copy(
            src, dst, pair_send.at[index], pair_recv.at[index], device_id=target, device_id_type=MESH
        )

    give = pair_copy(0, share.at[1 - core], share_in, sibling)
    cross = pair_copy(1, part, part_in, partner)
    finish = pair_copy(2, surf.at[core], surf.at[core], sibling)
    give.start()
    give.wait_recv()
    part[...] = share[core] + share_in[...]

    pl.when(far)(cross.start)

    await_halos(1)
    unpack_rows()

    @pl.when(folded)
    def _():
        fold_unpack(1)

    def other_slice(plane, carry):
        first_substep(plane)
        for block in range(ROWS // 8):
            updated[0, plane - 1, block * 8 : block * 8 + 8, :] = second_substep(plane, block)
        return carry

    lax.fori_loop(2, SLICES + 1, other_slice, 0)

    @pl.when(jnp.logical_not(far))
    def _():
        pl.semaphore_wait(ready, 1)
        cross.start()

    cross.wait_recv()
    surf[core] = part[...] + part_in[...]
    finish.start()

    finish.wait_recv()

    for block in range(ROWS // 8):
        rows = slice(block * 8, block * 8 + 8)
        ocean = jnp.concatenate([surf[0, rows, :], surf[1, rows, :]], axis=1)
        sea_new = ocean.astype(BF16).astype(F32)

        @pl.when(is_ocean)
        def _():
            updated[0, 0, rows, :] = ocean
            contrast[0, rows, :] = sea_new - seen[rows, :].astype(F32)

        @pl.when(jnp.logical_not(is_ocean))
        def _():
            contrast[0, rows, :] = sea_new - updated[0, 0, rows, :]

    await_sent(0)
    await_sent(1)
    give.wait_send()
    cross.wait_send()
    finish.wait_send()

    @pl.when(folded)
    def _():
        for away in range(1, n_lon):
            fold_copy(0, away).wait_send()
            fold_copy(1, away).wait_send()


def store(updated, contrast, updated_out, contrast_out, sem):
    copies = [
        pltpu.make_async_copy(contrast, contrast_out, sem.at[0]),
        pltpu.make_async_copy(updated, updated_out, sem.at[1]),
    ]
    for copy in copies:
        copy.start()
    for copy in copies:
        copy.wait()


def shards(n_lon, n_lat, *args):
    fields = args[0]
    vmem, sems = pltpu.VMEM, pltpu.SemaphoreType.DMA
    results = pl.pallas_call(
        functools.partial(kernel, n_lon, n_lat),
        out_shape=(
            pltpu.VMEM(fields.shape, F32),
            pltpu.VMEM((1, ROWS, COLS), F32),
        ),
        in_specs=[pl.BlockSpec(memory_space=pl.ANY)] * 8,
        out_specs=(pl.BlockSpec(memory_space=pltpu.VMEM),) * 2,
        scratch_shapes=[
            vmem((SLICES + 1, EXTR, EXTC), F32),
            vmem((SLICES, EXTR, EXTC), F32),
            vmem((ROWS, COLS), F32),
            vmem((ROWS, COLS), BF16),
            vmem((TAPS, ROWS, COLS), jnp.int32),
            vmem((TAPS, ROWS, COLS), F32),
            vmem((ROWS, COLS), jnp.int32),
            vmem((WIN * WIN, ROWS, COLS), F32),
            vmem((EXTR, EXTC), F32),
            vmem((WIN, EXTR, COLS), F32),
            vmem((2, ROWS, HALF), F32),
            vmem((ROWS, HALF), F32),
            vmem((ROWS, HALF), F32),
            vmem((ROWS, HALF), F32),
            vmem((2, ROWS, HALF), F32),
            vmem((2, PADR, COLS), F32),
            vmem((2, ROWS, PADC), F32),
            vmem((2, 16, COLS), F32),
            vmem((2, 16, COLS), F32),
            vmem((4, 8, PADC), F32),
            vmem((BLOCKS, 8, PADC), F32),
            vmem((BLOCKS, 16, PADC), F32),
            vmem((BLOCKS * n_lon, 8, PADC), F32),
            vmem((BLOCKS * n_lon, 16, PADC), F32),
            pltpu.SMEM((1024,), jnp.int32),
            sems((9,)),
            sems((2 * N_SIDES,)),
            sems((2 * N_SIDES,)),
            sems((3,)),
            sems((3,)),
            sems((2, n_lon)),
            sems((2, n_lon)),
            pltpu.SemaphoreType.REGULAR,
        ],
        compiler_params=pltpu.CompilerParams(
            collective_id=0, has_side_effects=True, vmem_limit_bytes=32 * 2**20
        ),
    )(*[pltpu.with_memory_space_constraint(a, pltpu.HBM) for a in args])
    return pl.pallas_call(
        store,
        out_shape=tuple(jax.ShapeDtypeStruct(r.shape, r.dtype) for r in results),
        in_specs=[pl.BlockSpec(memory_space=pltpu.VMEM)] * 2,
        out_specs=(pl.BlockSpec(memory_space=pl.ANY),) * 2,
        scratch_shapes=[sems((2,))],
    )(*[pltpu.with_memory_space_constraint(r, pltpu.VMEM) for r in results])


def solution(mesh):
    placed = (
        P("comp", None, "lat", "lon"),
        P("comp", "lat", "lon"),
        P("comp", "lat", "lon"),
        P("lat", "lon"),
        P(None, "lat", "lon"),
        P(None, "lat", "lon"),
        P("lat", "lon"),
        P(),
    )
    return jax.shard_map(
        functools.partial(shards, mesh.shape["lon"], mesh.shape["lat"]),
        mesh=mesh,
        in_specs=placed,
        out_specs=(P("comp", None, "lat", "lon"), P("comp", "lat", "lon")),
        check_vma=False,
    )
```

```python
import functools

import jax
import jax.numpy as jnp
from jax import lax
from jax.experimental import pallas as pl
from jax.experimental.pallas import tpu as pltpu
from jax.sharding import PartitionSpec as P

MESH = pl.DeviceIdType.MESH
F32, BF16 = jnp.float32, jnp.bfloat16
ROWS, COLS, SLICES, TAPS, WIN = 48, 512, 8, 8, 4
PADR, PADC = 8, 128
EXTR, EXTC = ROWS + 2 * PADR, COLS + 2 * PADC
HALF = COLS // 2
BLOCKS = COLS // PADC
N_SIDES = 8
AIR_GAIN = 0.5

MID_R, MID_C = pl.ds(PADR, ROWS), pl.ds(PADC, COLS)
LOW_R, HIGH_R = pl.ds(0, PADR), pl.ds(PADR + ROWS, PADR)
LOW_C, HIGH_C = pl.ds(0, PADC), pl.ds(PADC + COLS, PADC)
FIRST_R, LAST_R = pl.ds(PADR, PADR), pl.ds(ROWS, PADR)
FIRST_C, LAST_C = pl.ds(PADC, PADC), pl.ds(COLS, PADC)

SIDES = (
    (0, 1, LAST_R, MID_C, LOW_R, MID_C),
    (0, -1, FIRST_R, MID_C, HIGH_R, MID_C),
    (1, 0, MID_R, LAST_C, MID_R, LOW_C),
    (-1, 0, MID_R, FIRST_C, MID_R, HIGH_C),
    (1, 1, LAST_R, LAST_C, LOW_R, LOW_C),
    (-1, 1, LAST_R, FIRST_C, LOW_R, HIGH_C),
    (1, -1, FIRST_R, LAST_C, HIGH_R, LOW_C),
    (-1, -1, FIRST_R, FIRST_C, HIGH_R, HIGH_C),
)


FOLD_LINES = (
    ((1, 0, ROWS - 2), (1, 1, ROWS - 1), (0, 2, ROWS - 1)),
    tuple((plane, 8 * side + plane - 2, ROWS - 2 + side) for side in range(2) for plane in range(2, SLICES + 1)),
)


def roll(value, shift, axis):
    return pltpu.roll(value, shift % value.shape[axis], axis)


def kernel(
    n_lon,
    n_lat,
    fields,
    diffusion,
    exchange,
    sea_seen,
    code,
    weight,
    land,
    fold,
    updated,
    contrast,
    ext,
    mid,
    exch,
    seen,
    prior,
    codes,
    weights,
    sea_mask,
    chosen,
    padded,
    shifted,
    share,
    share_in,
    part,
    part_in,
    surf,
    edge_out,
    side_out,
    rows_out,
    rows_in,
    corner_in,
    fold_out_0,
    fold_out_1,
    fold_all_0,
    fold_all_1,
    fold_at,
    load_sem,
    halo_send,
    halo_recv,
    pair_send,
    pair_recv,
    fold_send,
    fold_recv,
    ready,
):
    lon, lat, comp = (lax.axis_index(a) for a in ("lon", "lat", "comp"))
    core = lax.rem(comp, 2)
    far = comp >= 2
    is_ocean = comp == 3
    folded = jnp.logical_and(is_ocean, lat == n_lat - 1)
    fold_out, fold_all = (fold_out_0, fold_out_1), (fold_all_0, fold_all_1)
    sibling = (lon, lat, comp + 1 - 2 * core)
    partner = (lon, lat, lax.rem(comp + 2, 4))

    def side_target(east, north):
        return (
            lax.rem(lon + east + n_lon, n_lon),
            lax.rem(lat + north + n_lat, n_lat),
            comp,
        )

    def has(north):
        if north == 0:
            return None
        return lat < n_lat - 1 if north > 0 else lat > 0

    def when(condition, action):
        if condition is None:
            action()
        else:
            pl.when(condition)(action)

    def local(src, dst, index):
        return pltpu.make_async_copy(src, dst, load_sem.at[index])

    loads = [
        local(diffusion.at[0], ext.at[0, MID_R, MID_C], 0),
        local(fields.at[0, 0], ext.at[1, MID_R, MID_C], 1),
        local(code, codes, 2),
        local(weight, weights, 3),
        local(sea_seen, seen, 4),
        local(exchange.at[0], exch, 5),
        local(land, sea_mask, 6),
        local(fields.at[0, pl.ds(1, SLICES - 1)], ext.at[pl.ds(2, SLICES - 1), MID_R, MID_C], 7),
    ]
    fold_load = local(fold.at[pl.ds(0, 1024)], fold_at, 8)
    barrier = pltpu.get_barrier_semaphore()

    def greet(target):
        pl.semaphore_signal(barrier, inc=1, device_id=target, device_id_type=MESH)

    for east, north, *_ in SIDES:
        when(has(north), functools.partial(greet, side_target(east, north)))
    greet(sibling)
    pl.when(jnp.logical_not(far))(functools.partial(greet, partner))

    @pl.when(folded)
    def _():
        fold_load.start()
        for away in range(1, n_lon):
            greet((lax.rem(lon + away, n_lon), lat, comp))

    for load in loads:
        load.start()

    @pl.when(lat == 0)
    def _():
        ext[:, 0:PADR, :] = jnp.zeros((SLICES + 1, PADR, EXTC), F32)

    @pl.when(lat == n_lat - 1)
    def _():
        ext[:, PADR + ROWS : EXTR, :] = jnp.zeros((SLICES + 1, PADR, EXTC), F32)

    def halo(group, index):
        east, north, src_r, src_c, dst_r, dst_c = SIDES[index]
        way = 0 if north > 0 else 1
        if group == 1 and index < 2:
            src, dst = rows_out.at[way], rows_in.at[way]
        elif group == 1 and index >= 4:
            cells = pl.ds(COLS - PADC, PADC) if east > 0 else pl.ds(0, PADC)
            src, dst = rows_out.at[way, pl.ds(8 - 8 * way, 8), cells], corner_in.at[index - 4]
        elif group == 0 and index < 2:
            src, dst = edge_out.at[way], ext.at[1, dst_r, dst_c]
        elif group == 0 and index < 4:
            src, dst = side_out.at[index - 2], ext.at[1, dst_r, dst_c]
        else:
            planes = pl.ds(2, SLICES - 1) if group == 1 else pl.ds(1, 1)
            src, dst = ext.at[planes, src_r, src_c], ext.at[planes, dst_r, dst_c]
        slot = group * N_SIDES + index
        return pltpu.make_async_remote_copy(
            src,
            dst,
            halo_send.at[slot],
            halo_recv.at[slot],
            device_id=side_target(east, north),
            device_id_type=MESH,
        )

    def pack_surface():
        line = lax.broadcasted_iota(jnp.int32, (PADR, COLS), 0)
        for way, at, spare, turn in ((0, ROWS, 0, 1), (1, PADR, PADR - 1, -1)):
            tile = ext[1, at : at + PADR, PADC : PADC + COLS]
            rate = ext[0, at : at + PADR, PADC : PADC + COLS]
            edge_out[way] = jnp.where(line == spare, roll(rate, turn, 0), tile)
        lane = lax.broadcasted_iota(jnp.int32, (ROWS, PADC), 1)
        for way, at, spare, turn in ((0, COLS, 0, 1), (1, PADC, PADC - 1, -1)):
            tile = ext[1, PADR : PADR + ROWS, at : at + PADC]
            rate = ext[0, PADR : PADR + ROWS, at : at + PADC]
            side_out[way] = jnp.where(lane == spare, roll(rate, turn, 1), tile)

    def unpack_surface():
        @pl.when(lat > 0)
        def _():
            ext[0, :PADR, PADC : PADC + COLS] = roll(ext[1, :PADR, PADC : PADC + COLS], -1, 0)

        @pl.when(lat < n_lat - 1)
        def _():
            beyond = slice(PADR + ROWS, EXTR)
            ext[0, beyond, PADC : PADC + COLS] = roll(ext[1, beyond, PADC : PADC + COLS], 1, 0)

        rows = slice(PADR, PADR + ROWS)
        ext[0, rows, :PADC] = roll(ext[1, rows, :PADC], -1, 1)
        ext[0, rows, PADC + COLS :] = roll(ext[1, rows, PADC + COLS :], 1, 1)

    def pack_rows():
        for plane in range(2, SLICES + 1):
            at = plane - 2
            tail = ext[plane, ROWS : ROWS + PADR, PADC : PADC + COLS]
            head = ext[plane, PADR : 2 * PADR, PADC : PADC + COLS]
            rows_out[0, at : at + 1, :] = tail[6:7]
            rows_out[0, 8 + at : 9 + at, :] = tail[7:8]
            rows_out[1, at : at + 1, :] = head[0:1]
            rows_out[1, 8 + at : 9 + at, :] = head[1:2]
        for way in range(2):
            for at in (7, 15):
                rows_out[way, at : at + 1, :] = jnp.zeros((1, COLS), F32)

    def unpack_rows():
        beyond = PADR + ROWS
        sides = (slice(0, PADC), slice(PADC + COLS, EXTC))

        @pl.when(lat > 0)
        def _():
            for plane in range(2, SLICES + 1):
                at = plane - 2
                ext[plane, PADR - 2 : PADR - 1, PADC : PADC + COLS] = rows_in[0, at : at + 1, :]
                ext[plane, PADR - 1 : PADR, PADC : PADC + COLS] = rows_in[0, 8 + at : 9 + at, :]
                for side in range(2):
                    ext[plane, PADR - 1 : PADR, sides[side]] = corner_in[side, at : at + 1, :]

        @pl.when(lat < n_lat - 1)
        def _():
            for plane in range(2, SLICES + 1):
                at = plane - 2
                ext[plane, beyond : beyond + 1, PADC : PADC + COLS] = rows_in[1, at : at + 1, :]
                ext[plane, beyond + 1 : beyond + 2, PADC : PADC + COLS] = rows_in[1, 8 + at : 9 + at, :]
                for side in range(2):
                    ext[plane, beyond : beyond + 1, sides[side]] = corner_in[2 + side, at : at + 1, :]

    def send_halos(group):
        for index in reversed(range(N_SIDES)):
            when(has(SIDES[index][1]), halo(group, index).start)

    def await_halos(group):
        for index in range(N_SIDES):
            when(has(-SIDES[index][1]), halo(group, index).wait_recv)

    def await_sent(group):
        for index in range(N_SIDES):
            when(has(SIDES[index][1]), halo(group, index).wait_send)

    loads[0].wait()
    loads[1].wait()
    pack_surface()
    expected = (
        3
        + 3 * (lat > 0).astype(jnp.int32)
        + 3 * (lat < n_lat - 1).astype(jnp.int32)
        + far.astype(jnp.int32)
        + (n_lon - 1) * folded.astype(jnp.int32)
    )
    pl.semaphore_wait(barrier, expected)

    @pl.when(far)
    def _():
        pl.semaphore_signal(ready, inc=1, device_id=partner, device_id_type=MESH)

    send_halos(0)

    def fold_copy(group, away):
        return pltpu.make_async_remote_copy(
            fold_out[group],
            fold_all[group].at[pl.ds(BLOCKS * lon, BLOCKS)],
            fold_send.at[group, away],
            fold_recv.at[group, away],
            device_id=(lax.rem(lon + away, n_lon), lat, comp),
            device_id_type=MESH,
        )

    def fold_pack(group):
        for block in range(BLOCKS):
            cols = slice(PADC + block * PADC, 2 * PADC + block * PADC)
            for plane, at, row in FOLD_LINES[group]:
                fold_out[group][block, at : at + 1, :] = ext[plane, PADR + row : PADR + row + 1, cols]
        fold_all[group][pl.ds(BLOCKS * lon, BLOCKS)] = fold_out[group][...]
        for away in range(1, n_lon):
            fold_copy(group, away).start()

    def fold_unpack(group):
        for away in range(1, n_lon):
            fold_copy(group, away).wait_recv()
        ahead = fold_at[0] + n_lon * COLS - (lon + 1) * COLS
        start = ahead // PADC
        rest = lax.rem(ahead, PADC)
        window = [fold_all[group][lax.rem(start + i, BLOCKS * n_lon)] for i in range(BLOCKS + 2)]
        spots = lax.broadcasted_iota(jnp.int32, (2 * PADC, PADC), 0) + lax.broadcasted_iota(
            jnp.int32, (2 * PADC, PADC), 1
        )
        pick = jnp.where(spots == PADC + rest, 1.0, 0.0).astype(F32)
        for block in range(BLOCKS + 2):
            pair = jnp.concatenate([window[max(BLOCKS - block, 0)], window[BLOCKS + 1 - block]], axis=1)
            mirrored = jnp.dot(
                pair, pick, precision=lax.Precision.HIGHEST, preferred_element_type=F32
            )
            cols = slice(block * PADC, (block + 1) * PADC)
            for plane, at, row in FOLD_LINES[group]:
                to = PADR + 2 * ROWS - 1 - row
                ext[plane, to : to + 1, cols] = mirrored[at : at + 1]

    @pl.when(folded)
    def _():
        for packed in fold_out:
            packed[...] = jnp.zeros(packed.shape, F32)
        fold_pack(0)

    loads[7].wait()
    pack_rows()
    send_halos(1)

    @pl.when(folded)
    def _():
        fold_pack(1)

    loads[2].wait()
    loads[3].wait()
    loads[4].wait()
    loads[5].wait()
    loads[6].wait()
    for at in range(0, ROWS, 16):
        prior[at : at + 16, :] = seen[at : at + 16, :].astype(F32)

    @pl.when(jnp.logical_not(is_ocean))
    def _():
        first = comp * (WIN * WIN)

        def rows_of(step, carry):
            at = pl.multiple_of(step * 8, 8)
            for block in range(BLOCKS):
                cols = slice(block * PADC, (block + 1) * PADC)
                tap_code = [codes[tap, pl.ds(at, 8), cols] - first for tap in range(TAPS)]
                tap_weight = [weights[tap, pl.ds(at, 8), cols] for tap in range(TAPS)]
                for cell in range(WIN * WIN):
                    terms = [jnp.where(c == cell, w, 0.0) for c, w in zip(tap_code, tap_weight)]
                    while len(terms) > 1:
                        terms = [a + b for a, b in zip(terms[::2], terms[1::2])]
                    chosen[cell, pl.ds(at, 8), cols] = terms[0]
            return carry

        lax.fori_loop(0, ROWS // 8, rows_of, 0)

    def first_substep(plane):
        for block in range(EXTR // 8):
            at = block * 8
            here = ext[plane, at : at + 8, :]
            if block < EXTR // 8 - 1:
                north = ext[plane, at + 1 : at + 9, :]
            else:
                north = roll(here, -1, 0)
            if block > 0:
                south = ext[plane, at - 1 : at + 7, :]
            else:
                south = roll(here, 1, 0)
            east, west = roll(here, -1, 1), roll(here, 1, 1)
            rate = ext[0, at : at + 8, :]
            mid[plane - 1, at : at + 8, :] = here + rate * (north + south + east + west - 4.0 * here)

    def second_substep(plane, block):
        at = PADR + block * 8
        whole = mid[plane - 1, at : at + 8, :]
        here = whole[:, PADC : PADC + COLS]
        north = mid[plane - 1, at + 1 : at + 9, PADC : PADC + COLS]
        south = mid[plane - 1, at - 1 : at + 7, PADC : PADC + COLS]
        east = roll(whole, -1, 1)[:, PADC : PADC + COLS]
        west = roll(whole, 1, 1)[:, PADC : PADC + COLS]
        rate = ext[0, at : at + 8, PADC : PADC + COLS]
        return here + rate * (north + south + east + west - 4.0 * here)

    await_halos(0)
    unpack_surface()

    @pl.when(folded)
    def _():
        fold_load.wait()
        fold_unpack(0)

    first_substep(1)

    @pl.when(is_ocean)
    def _():
        for block in range(ROWS // 8):
            rows = slice(block * 8, block * 8 + 8)
            lowest = second_substep(1, block)
            share[0, rows, :] = lowest[:, :HALF]
            share[1, rows, :] = lowest[:, HALF:]

    @pl.when(jnp.logical_not(is_ocean))
    def _():
        for block in range(ROWS // 8):
            rows = slice(block * 8, block * 8 + 8)
            lowest = second_substep(1, block)
            flux = exch[rows, :] * (prior[rows, :] - lowest)
            flux = flux.astype(BF16).astype(F32)
            updated[0, 0, rows, :] = lowest + AIR_GAIN * flux
            at = PADR + block * 8
            padded[at : at + 8, PADC : PADC + COLS] = flux
            padded[at : at + 8, :PADC] = jnp.broadcast_to(flux[:, :1], (8, PADC))
            padded[at : at + 8, PADC + COLS :] = jnp.broadcast_to(flux[:, COLS - 1 :], (8, PADC))
        padded[:PADR, :] = jnp.broadcast_to(padded[PADR : PADR + 1, :], (PADR, EXTC))
        end = PADR + ROWS
        padded[end:, :] = jnp.broadcast_to(padded[end - 1 : end, :], (PADR, EXTC))
        for block in range(EXTR // 8):
            at = block * 8
            whole = padded[at : at + 8, :]
            for step in range(WIN):
                shifted[step, at : at + 8, :] = roll(whole, 1 - step, 1)[:, PADC : PADC + COLS]
        for block in range(ROWS // 8):
            rows = slice(block * 8, block * 8 + 8)
            total = None
            for step in range(WIN):
                for up in range(WIN):
                    at = PADR + block * 8 + up - 1
                    term = chosen[WIN * up + step, rows, :] * shifted[step, at : at + 8, :]
                    total = term if total is None else total + term
            total = total * (sea_mask[rows, :].astype(F32) * (1.0 / 3.0))
            share[0, rows, :] = total[:, :HALF]
            share[1, rows, :] = total[:, HALF:]

    def pair_copy(index, src, dst, target):
        return pltpu.make_async_remote_copy(
            src, dst, pair_send.at[index], pair_recv.at[index], device_id=target, device_id_type=MESH
        )

    give = pair_copy(0, share.at[1 - core], share_in, sibling)
    cross = pair_copy(1, part, part_in, partner)
    finish = pair_copy(2, surf.at[core], surf.at[core], sibling)
    give.start()
    give.wait_recv()
    part[...] = share[core] + share_in[...]

    pl.when(far)(cross.start)

    await_halos(1)
    unpack_rows()

    @pl.when(folded)
    def _():
        fold_unpack(1)

    def other_slice(plane, carry):
        first_substep(plane)
        for block in range(ROWS // 8):
            updated[0, plane - 1, block * 8 : block * 8 + 8, :] = second_substep(plane, block)
        return carry

    lax.fori_loop(2, SLICES + 1, other_slice, 0)

    @pl.when(jnp.logical_not(far))
    def _():
        pl.semaphore_wait(ready, 1)
        cross.start()

    cross.wait_recv()
    surf[core] = part[...] + part_in[...]
    finish.start()

    finish.wait_recv()

    for block in range(ROWS // 8):
        rows = slice(block * 8, block * 8 + 8)
        ocean = jnp.concatenate([surf[0, rows, :], surf[1, rows, :]], axis=1)
        sea_new = ocean.astype(BF16).astype(F32)

        @pl.when(is_ocean)
        def _():
            updated[0, 0, rows, :] = ocean
            contrast[0, rows, :] = sea_new - prior[rows, :]

        @pl.when(jnp.logical_not(is_ocean))
        def _():
            contrast[0, rows, :] = sea_new - updated[0, 0, rows, :]

    await_sent(0)
    await_sent(1)
    give.wait_send()
    cross.wait_send()
    finish.wait_send()

    @pl.when(folded)
    def _():
        for away in range(1, n_lon):
            fold_copy(0, away).wait_send()
            fold_copy(1, away).wait_send()


def store(updated, contrast, updated_out, contrast_out, sem):
    copies = [
        pltpu.make_async_copy(contrast, contrast_out, sem.at[0]),
        pltpu.make_async_copy(updated, updated_out, sem.at[1]),
    ]
    for copy in copies:
        copy.start()
    for copy in copies:
        copy.wait()


def shards(n_lon, n_lat, *args):
    fields = args[0]
    vmem, sems = pltpu.VMEM, pltpu.SemaphoreType.DMA
    results = pl.pallas_call(
        functools.partial(kernel, n_lon, n_lat),
        out_shape=(
            pltpu.VMEM(fields.shape, F32),
            pltpu.VMEM((1, ROWS, COLS), F32),
        ),
        in_specs=[pl.BlockSpec(memory_space=pl.ANY)] * 8,
        out_specs=(pl.BlockSpec(memory_space=pltpu.VMEM),) * 2,
        scratch_shapes=[
            vmem((SLICES + 1, EXTR, EXTC), F32),
            vmem((SLICES, EXTR, EXTC), F32),
            vmem((ROWS, COLS), F32),
            vmem((ROWS, COLS), BF16),
            vmem((ROWS, COLS), F32),
            vmem((TAPS, ROWS, COLS), jnp.int32),
            vmem((TAPS, ROWS, COLS), F32),
            vmem((ROWS, COLS), jnp.int32),
            vmem((WIN * WIN, ROWS, COLS), F32),
            vmem((EXTR, EXTC), F32),
            vmem((WIN, EXTR, COLS), F32),
            vmem((2, ROWS, HALF), F32),
            vmem((ROWS, HALF), F32),
            vmem((ROWS, HALF), F32),
            vmem((ROWS, HALF), F32),
            vmem((2, ROWS, HALF), F32),
            vmem((2, PADR, COLS), F32),
            vmem((2, ROWS, PADC), F32),
            vmem((2, 16, COLS), F32),
            vmem((2, 16, COLS), F32),
            vmem((4, 8, PADC), F32),
            vmem((BLOCKS, 8, PADC), F32),
            vmem((BLOCKS, 16, PADC), F32),
            vmem((BLOCKS * n_lon, 8, PADC), F32),
            vmem((BLOCKS * n_lon, 16, PADC), F32),
            pltpu.SMEM((1024,), jnp.int32),
            sems((9,)),
            sems((2 * N_SIDES,)),
            sems((2 * N_SIDES,)),
            sems((3,)),
            sems((3,)),
            sems((2, n_lon)),
            sems((2, n_lon)),
            pltpu.SemaphoreType.REGULAR,
        ],
        compiler_params=pltpu.CompilerParams(
            collective_id=0, has_side_effects=True, vmem_limit_bytes=32 * 2**20
        ),
    )(*[pltpu.with_memory_space_constraint(a, pltpu.HBM) for a in args])
    return pl.pallas_call(
        store,
        out_shape=tuple(jax.ShapeDtypeStruct(r.shape, r.dtype) for r in results),
        in_specs=[pl.BlockSpec(memory_space=pltpu.VMEM)] * 2,
        out_specs=(pl.BlockSpec(memory_space=pl.ANY),) * 2,
        scratch_shapes=[sems((2,))],
    )(*[pltpu.with_memory_space_constraint(r, pltpu.VMEM) for r in results])


def solution(mesh):
    placed = (
        P("comp", None, "lat", "lon"),
        P("comp", "lat", "lon"),
        P("comp", "lat", "lon"),
        P("lat", "lon"),
        P(None, "lat", "lon"),
        P(None, "lat", "lon"),
        P("lat", "lon"),
        P(),
    )
    return jax.shard_map(
        functools.partial(shards, mesh.shape["lon"], mesh.shape["lat"]),
        mesh=mesh,
        in_specs=placed,
        out_specs=(P("comp", None, "lat", "lon"), P("comp", "lat", "lon")),
        check_vma=False,
    )
```

```python
import functools

import jax
import jax.numpy as jnp
from jax import lax
from jax.experimental import pallas as pl
from jax.experimental.pallas import tpu as pltpu
from jax.sharding import PartitionSpec as P

MESH = pl.DeviceIdType.MESH
F32, BF16 = jnp.float32, jnp.bfloat16
ROWS, COLS, SLICES, TAPS, WIN = 48, 512, 8, 8, 4
PADR, PADC = 8, 128
EXTR, EXTC = ROWS + 2 * PADR, COLS + 2 * PADC
HALF = COLS // 2
CHUNKS = (pl.ds(0, 32), pl.ds(32, 16))
BLOCKS = COLS // PADC
N_SIDES = 8
AIR_GAIN = 0.5

MID_R, MID_C = pl.ds(PADR, ROWS), pl.ds(PADC, COLS)
LOW_R, HIGH_R = pl.ds(0, PADR), pl.ds(PADR + ROWS, PADR)
LOW_C, HIGH_C = pl.ds(0, PADC), pl.ds(PADC + COLS, PADC)
FIRST_R, LAST_R = pl.ds(PADR, PADR), pl.ds(ROWS, PADR)
FIRST_C, LAST_C = pl.ds(PADC, PADC), pl.ds(COLS, PADC)

SIDES = (
    (0, 1, LAST_R, MID_C, LOW_R, MID_C),
    (0, -1, FIRST_R, MID_C, HIGH_R, MID_C),
    (1, 0, MID_R, LAST_C, MID_R, LOW_C),
    (-1, 0, MID_R, FIRST_C, MID_R, HIGH_C),
    (1, 1, LAST_R, LAST_C, LOW_R, LOW_C),
    (-1, 1, LAST_R, FIRST_C, LOW_R, HIGH_C),
    (1, -1, FIRST_R, LAST_C, HIGH_R, LOW_C),
    (-1, -1, FIRST_R, FIRST_C, HIGH_R, HIGH_C),
)


FOLD_LINES = (
    ((1, 0, ROWS - 2), (1, 1, ROWS - 1), (0, 2, ROWS - 1)),
    tuple((plane, 8 * side + plane - 2, ROWS - 2 + side) for side in range(2) for plane in range(2, SLICES + 1)),
)


def roll(value, shift, axis):
    return pltpu.roll(value, shift % value.shape[axis], axis)


def kernel(
    n_lon,
    n_lat,
    fields,
    diffusion,
    exchange,
    sea_seen,
    code,
    weight,
    land,
    fold,
    updated,
    contrast,
    ext,
    mid,
    exch,
    seen,
    prior,
    codes,
    weights,
    sea_mask,
    chosen,
    padded,
    shifted,
    share,
    share_in,
    part,
    part_in,
    surf,
    edge_out,
    side_out,
    rows_out,
    rows_in,
    corner_in,
    fold_out_0,
    fold_out_1,
    fold_all_0,
    fold_all_1,
    fold_at,
    load_sem,
    halo_send,
    halo_recv,
    pair_send,
    pair_recv,
    fold_send,
    fold_recv,
    ready,
):
    lon, lat, comp = (lax.axis_index(a) for a in ("lon", "lat", "comp"))
    core = lax.rem(comp, 2)
    far = comp >= 2
    is_ocean = comp == 3
    folded = jnp.logical_and(is_ocean, lat == n_lat - 1)
    fold_out, fold_all = (fold_out_0, fold_out_1), (fold_all_0, fold_all_1)
    sibling = (lon, lat, comp + 1 - 2 * core)
    partner = (lon, lat, lax.rem(comp + 2, 4))

    def side_target(east, north):
        return (
            lax.rem(lon + east + n_lon, n_lon),
            lax.rem(lat + north + n_lat, n_lat),
            comp,
        )

    def has(north):
        if north == 0:
            return None
        return lat < n_lat - 1 if north > 0 else lat > 0

    def when(condition, action):
        if condition is None:
            action()
        else:
            pl.when(condition)(action)

    def local(src, dst, index):
        return pltpu.make_async_copy(src, dst, load_sem.at[index])

    loads = [
        local(diffusion.at[0], ext.at[0, MID_R, MID_C], 0),
        local(fields.at[0, 0], ext.at[1, MID_R, MID_C], 1),
        local(code, codes, 2),
        local(weight, weights, 3),
        local(sea_seen, seen, 4),
        local(exchange.at[0], exch, 5),
        local(land, sea_mask, 6),
        local(fields.at[0, pl.ds(1, SLICES - 1)], ext.at[pl.ds(2, SLICES - 1), MID_R, MID_C], 7),
    ]
    fold_load = local(fold.at[pl.ds(0, 1024)], fold_at, 8)
    loads[0].start()
    loads[1].start()

    barrier = pltpu.get_barrier_semaphore()

    def greet(target):
        pl.semaphore_signal(barrier, inc=1, device_id=target, device_id_type=MESH)

    for east, north, *_ in reversed(SIDES):
        when(has(north), functools.partial(greet, side_target(east, north)))
    greet(sibling)
    pl.when(jnp.logical_not(far))(functools.partial(greet, partner))

    @pl.when(folded)
    def _():
        fold_load.start()
        for away in range(1, n_lon):
            greet((lax.rem(lon + away, n_lon), lat, comp))

    for load in loads[2:]:
        load.start()

    @pl.when(lat == 0)
    def _():
        ext[:, 0:PADR, :] = jnp.zeros((SLICES + 1, PADR, EXTC), F32)

    @pl.when(lat == n_lat - 1)
    def _():
        ext[:, PADR + ROWS : EXTR, :] = jnp.zeros((SLICES + 1, PADR, EXTC), F32)

    def halo(group, index):
        east, north, src_r, src_c, dst_r, dst_c = SIDES[index]
        way = 0 if north > 0 else 1
        if group == 1 and index < 2:
            src, dst = rows_out.at[way], rows_in.at[way]
        elif group == 1 and index >= 4:
            cells = pl.ds(COLS - PADC, PADC) if east > 0 else pl.ds(0, PADC)
            src, dst = rows_out.at[way, pl.ds(8 - 8 * way, 8), cells], corner_in.at[index - 4]
        elif group == 0 and index >= 4:
            rows = pl.ds(ROWS - PADR, PADR) if north > 0 else pl.ds(0, PADR)
            cols = pl.ds(COLS - PADC, PADC) if east > 0 else pl.ds(0, PADC)
            src, dst = fields.at[0, 0, rows, cols], ext.at[1, dst_r, dst_c]
        elif group == 0 and index < 2:
            src, dst = edge_out.at[way], ext.at[1, dst_r, dst_c]
        elif group == 0 and index < 4:
            src, dst = side_out.at[index - 2], ext.at[1, dst_r, dst_c]
        else:
            src, dst = ext.at[pl.ds(2, SLICES - 1), src_r, src_c], ext.at[pl.ds(2, SLICES - 1), dst_r, dst_c]
        slot = group * N_SIDES + index
        return pltpu.make_async_remote_copy(
            src,
            dst,
            halo_send.at[slot],
            halo_recv.at[slot],
            device_id=side_target(east, north),
            device_id_type=MESH,
        )

    def pack_surface():
        line = lax.broadcasted_iota(jnp.int32, (PADR, COLS), 0)
        for way, at, spare, turn in ((0, ROWS, 0, 1), (1, PADR, PADR - 1, -1)):
            tile = ext[1, at : at + PADR, PADC : PADC + COLS]
            rate = ext[0, at : at + PADR, PADC : PADC + COLS]
            edge_out[way] = jnp.where(line == spare, roll(rate, turn, 0), tile)
        lane = lax.broadcasted_iota(jnp.int32, (ROWS, PADC), 1)
        for way, at, spare, turn in ((0, COLS, 0, 1), (1, PADC, PADC - 1, -1)):
            tile = ext[1, PADR : PADR + ROWS, at : at + PADC]
            rate = ext[0, PADR : PADR + ROWS, at : at + PADC]
            side_out[way] = jnp.where(lane == spare, roll(rate, turn, 1), tile)

    def unpack_surface():
        @pl.when(lat > 0)
        def _():
            ext[0, :PADR, PADC : PADC + COLS] = roll(ext[1, :PADR, PADC : PADC + COLS], -1, 0)

        @pl.when(lat < n_lat - 1)
        def _():
            beyond = slice(PADR + ROWS, EXTR)
            ext[0, beyond, PADC : PADC + COLS] = roll(ext[1, beyond, PADC : PADC + COLS], 1, 0)

        rows = slice(PADR, PADR + ROWS)
        ext[0, rows, :PADC] = roll(ext[1, rows, :PADC], -1, 1)
        ext[0, rows, PADC + COLS :] = roll(ext[1, rows, PADC + COLS :], 1, 1)

    def pack_rows():
        for plane in range(2, SLICES + 1):
            at = plane - 2
            tail = ext[plane, ROWS : ROWS + PADR, PADC : PADC + COLS]
            head = ext[plane, PADR : 2 * PADR, PADC : PADC + COLS]
            rows_out[0, at : at + 1, :] = tail[6:7]
            rows_out[0, 8 + at : 9 + at, :] = tail[7:8]
            rows_out[1, at : at + 1, :] = head[0:1]
            rows_out[1, 8 + at : 9 + at, :] = head[1:2]
        for way in range(2):
            for at in (7, 15):
                rows_out[way, at : at + 1, :] = jnp.zeros((1, COLS), F32)

    def unpack_rows():
        beyond = PADR + ROWS
        sides = (slice(0, PADC), slice(PADC + COLS, EXTC))

        @pl.when(lat > 0)
        def _():
            for plane in range(2, SLICES + 1):
                at = plane - 2
                ext[plane, PADR - 2 : PADR - 1, PADC : PADC + COLS] = rows_in[0, at : at + 1, :]
                ext[plane, PADR - 1 : PADR, PADC : PADC + COLS] = rows_in[0, 8 + at : 9 + at, :]
                for side in range(2):
                    ext[plane, PADR - 1 : PADR, sides[side]] = corner_in[side, at : at + 1, :]

        @pl.when(lat < n_lat - 1)
        def _():
            for plane in range(2, SLICES + 1):
                at = plane - 2
                ext[plane, beyond : beyond + 1, PADC : PADC + COLS] = rows_in[1, at : at + 1, :]
                ext[plane, beyond + 1 : beyond + 2, PADC : PADC + COLS] = rows_in[1, 8 + at : 9 + at, :]
                for side in range(2):
                    ext[plane, beyond : beyond + 1, sides[side]] = corner_in[2 + side, at : at + 1, :]

    def send_halos(group, order):
        for index in order:
            when(has(SIDES[index][1]), halo(group, index).start)

    def await_halos(group):
        for index in range(N_SIDES):
            when(has(-SIDES[index][1]), halo(group, index).wait_recv)

    def await_sent(group):
        for index in range(N_SIDES):
            when(has(SIDES[index][1]), halo(group, index).wait_send)

    expected = (
        3
        + 3 * (lat > 0).astype(jnp.int32)
        + 3 * (lat < n_lat - 1).astype(jnp.int32)
        + far.astype(jnp.int32)
        + (n_lon - 1) * folded.astype(jnp.int32)
    )
    pl.semaphore_wait(barrier, expected)

    @pl.when(far)
    def _():
        pl.semaphore_signal(ready, inc=1, device_id=partner, device_id_type=MESH)

    send_halos(0, range(4, N_SIDES))
    loads[0].wait()
    loads[1].wait()
    pack_surface()
    send_halos(0, (2, 3, 0, 1))

    def fold_copy(group, away):
        return pltpu.make_async_remote_copy(
            fold_out[group],
            fold_all[group].at[pl.ds(BLOCKS * lon, BLOCKS)],
            fold_send.at[group, away],
            fold_recv.at[group, away],
            device_id=(lax.rem(lon + away, n_lon), lat, comp),
            device_id_type=MESH,
        )

    def fold_pack(group):
        for block in range(BLOCKS):
            cols = slice(PADC + block * PADC, 2 * PADC + block * PADC)
            for plane, at, row in FOLD_LINES[group]:
                fold_out[group][block, at : at + 1, :] = ext[plane, PADR + row : PADR + row + 1, cols]
        fold_all[group][pl.ds(BLOCKS * lon, BLOCKS)] = fold_out[group][...]
        for away in range(1, n_lon):
            fold_copy(group, away).start()

    def fold_unpack(group):
        for away in range(1, n_lon):
            fold_copy(group, away).wait_recv()
        ahead = fold_at[0] + n_lon * COLS - (lon + 1) * COLS
        start = ahead // PADC
        rest = lax.rem(ahead, PADC)
        window = [fold_all[group][lax.rem(start + i, BLOCKS * n_lon)] for i in range(BLOCKS + 2)]
        spots = lax.broadcasted_iota(jnp.int32, (2 * PADC, PADC), 0) + lax.broadcasted_iota(
            jnp.int32, (2 * PADC, PADC), 1
        )
        pick = jnp.where(spots == PADC + rest, 1.0, 0.0).astype(F32)
        for block in range(BLOCKS + 2):
            pair = jnp.concatenate([window[max(BLOCKS - block, 0)], window[BLOCKS + 1 - block]], axis=1)
            mirrored = jnp.dot(
                pair, pick, precision=lax.Precision.HIGHEST, preferred_element_type=F32
            )
            cols = slice(block * PADC, (block + 1) * PADC)
            for plane, at, row in FOLD_LINES[group]:
                to = PADR + 2 * ROWS - 1 - row
                ext[plane, to : to + 1, cols] = mirrored[at : at + 1]

    @pl.when(folded)
    def _():
        for packed in fold_out:
            packed[...] = jnp.zeros(packed.shape, F32)
        fold_pack(0)

    loads[7].wait()
    pack_rows()
    send_halos(1, range(N_SIDES))

    @pl.when(folded)
    def _():
        fold_pack(1)

    loads[2].wait()
    loads[3].wait()
    loads[4].wait()
    loads[5].wait()
    loads[6].wait()
    for at in range(0, ROWS, 16):
        prior[at : at + 16, :] = seen[at : at + 16, :].astype(F32)

    @pl.when(jnp.logical_not(is_ocean))
    def _():
        first = comp * (WIN * WIN)

        def rows_of(step, carry):
            at = pl.multiple_of(step * 8, 8)
            for block in range(BLOCKS):
                cols = slice(block * PADC, (block + 1) * PADC)
                tap_code = [codes[tap, pl.ds(at, 8), cols] - first for tap in range(TAPS)]
                tap_weight = [weights[tap, pl.ds(at, 8), cols] for tap in range(TAPS)]
                for cell in range(WIN * WIN):
                    terms = [jnp.where(c == cell, w, 0.0) for c, w in zip(tap_code, tap_weight)]
                    while len(terms) > 1:
                        terms = [a + b for a, b in zip(terms[::2], terms[1::2])]
                    chosen[cell, pl.ds(at, 8), cols] = terms[0]
            return carry

        lax.fori_loop(0, ROWS // 8, rows_of, 0)

    def first_substep(plane):
        for block in range(EXTR // 8):
            at = block * 8
            here = ext[plane, at : at + 8, :]
            if block < EXTR // 8 - 1:
                north = ext[plane, at + 1 : at + 9, :]
            else:
                north = roll(here, -1, 0)
            if block > 0:
                south = ext[plane, at - 1 : at + 7, :]
            else:
                south = roll(here, 1, 0)
            east, west = roll(here, -1, 1), roll(here, 1, 1)
            rate = ext[0, at : at + 8, :]
            mid[plane - 1, at : at + 8, :] = here + rate * (north + south + east + west - 4.0 * here)

    def second_substep(plane, block):
        at = PADR + block * 8
        whole = mid[plane - 1, at : at + 8, :]
        here = whole[:, PADC : PADC + COLS]
        north = mid[plane - 1, at + 1 : at + 9, PADC : PADC + COLS]
        south = mid[plane - 1, at - 1 : at + 7, PADC : PADC + COLS]
        east = roll(whole, -1, 1)[:, PADC : PADC + COLS]
        west = roll(whole, 1, 1)[:, PADC : PADC + COLS]
        rate = ext[0, at : at + 8, PADC : PADC + COLS]
        return here + rate * (north + south + east + west - 4.0 * here)

    await_halos(0)
    unpack_surface()

    @pl.when(folded)
    def _():
        fold_load.wait()
        fold_unpack(0)

    first_substep(1)

    @pl.when(is_ocean)
    def _():
        for block in range(ROWS // 8):
            rows = slice(block * 8, block * 8 + 8)
            lowest = second_substep(1, block)
            share[0, rows, :] = lowest[:, :HALF]
            share[1, rows, :] = lowest[:, HALF:]

    @pl.when(jnp.logical_not(is_ocean))
    def _():
        for block in range(ROWS // 8):
            rows = slice(block * 8, block * 8 + 8)
            lowest = second_substep(1, block)
            flux = exch[rows, :] * (prior[rows, :] - lowest)
            flux = flux.astype(BF16).astype(F32)
            updated[0, 0, rows, :] = lowest + AIR_GAIN * flux
            at = PADR + block * 8
            padded[at : at + 8, PADC : PADC + COLS] = flux
            padded[at : at + 8, :PADC] = jnp.broadcast_to(flux[:, :1], (8, PADC))
            padded[at : at + 8, PADC + COLS :] = jnp.broadcast_to(flux[:, COLS - 1 :], (8, PADC))
        padded[:PADR, :] = jnp.broadcast_to(padded[PADR : PADR + 1, :], (PADR, EXTC))
        end = PADR + ROWS
        padded[end:, :] = jnp.broadcast_to(padded[end - 1 : end, :], (PADR, EXTC))
        for block in range(EXTR // 8):
            at = block * 8
            whole = padded[at : at + 8, :]
            for step in range(WIN):
                shifted[step, at : at + 8, :] = roll(whole, 1 - step, 1)[:, PADC : PADC + COLS]
        for block in range(ROWS // 8):
            rows = slice(block * 8, block * 8 + 8)
            total = None
            for step in range(WIN):
                for up in range(WIN):
                    at = PADR + block * 8 + up - 1
                    term = chosen[WIN * up + step, rows, :] * shifted[step, at : at + 8, :]
                    total = term if total is None else total + term
            total = total * (sea_mask[rows, :].astype(F32) * (1.0 / 3.0))
            share[0, rows, :] = total[:, :HALF]
            share[1, rows, :] = total[:, HALF:]

    def pair_copy(index, src, dst, target):
        return pltpu.make_async_remote_copy(
            src, dst, pair_send.at[index], pair_recv.at[index], device_id=target, device_id_type=MESH
        )

    give = pair_copy(0, share.at[1 - core], share_in, sibling)
    cross = [pair_copy(1 + i, part.at[c], part_in.at[c], partner) for i, c in enumerate(CHUNKS)]
    finish = [pair_copy(3 + i, surf.at[core, c], surf.at[core, c], sibling) for i, c in enumerate(CHUNKS)]

    def start_cross():
        for piece in cross:
            piece.start()

    give.start()
    give.wait_recv()
    part[...] = share[core] + share_in[...]

    pl.when(far)(start_cross)

    await_halos(1)
    unpack_rows()

    @pl.when(folded)
    def _():
        fold_unpack(1)

    def other_slice(plane, carry):
        first_substep(plane)
        for block in range(ROWS // 8):
            updated[0, plane - 1, block * 8 : block * 8 + 8, :] = second_substep(plane, block)
        return carry

    lax.fori_loop(2, SLICES + 1, other_slice, 0)

    @pl.when(jnp.logical_not(far))
    def _():
        pl.semaphore_wait(ready, 1)
        start_cross()

    for piece, chunk in enumerate(CHUNKS):
        cross[piece].wait_recv()
        surf[core, chunk] = part[chunk] + part_in[chunk]
        finish[piece].start()

    for piece, chunk in enumerate(CHUNKS):
        finish[piece].wait_recv()
        for at in range(chunk.start, chunk.start + chunk.size, 8):
            rows = slice(at, at + 8)
            ocean = jnp.concatenate([surf[0, rows, :], surf[1, rows, :]], axis=1)
            sea_new = ocean.astype(BF16).astype(F32)

            @pl.when(is_ocean)
            def _():
                updated[0, 0, rows, :] = ocean
                contrast[0, rows, :] = sea_new - prior[rows, :]

            @pl.when(jnp.logical_not(is_ocean))
            def _():
                contrast[0, rows, :] = sea_new - updated[0, 0, rows, :]

    await_sent(0)
    await_sent(1)
    give.wait_send()
    for piece in cross + finish:
        piece.wait_send()

    @pl.when(folded)
    def _():
        for away in range(1, n_lon):
            fold_copy(0, away).wait_send()
            fold_copy(1, away).wait_send()


def store(updated, contrast, updated_out, contrast_out, sem):
    copies = [
        pltpu.make_async_copy(contrast, contrast_out, sem.at[0]),
        pltpu.make_async_copy(updated, updated_out, sem.at[1]),
    ]
    for copy in copies:
        copy.start()
    for copy in copies:
        copy.wait()


def shards(n_lon, n_lat, *args):
    fields = args[0]
    vmem, sems = pltpu.VMEM, pltpu.SemaphoreType.DMA
    results = pl.pallas_call(
        functools.partial(kernel, n_lon, n_lat),
        out_shape=(
            pltpu.VMEM(fields.shape, F32),
            pltpu.VMEM((1, ROWS, COLS), F32),
        ),
        in_specs=[pl.BlockSpec(memory_space=pl.ANY)] * 8,
        out_specs=(pl.BlockSpec(memory_space=pltpu.VMEM),) * 2,
        scratch_shapes=[
            vmem((SLICES + 1, EXTR, EXTC), F32),
            vmem((SLICES, EXTR, EXTC), F32),
            vmem((ROWS, COLS), F32),
            vmem((ROWS, COLS), BF16),
            vmem((ROWS, COLS), F32),
            vmem((TAPS, ROWS, COLS), jnp.int32),
            vmem((TAPS, ROWS, COLS), F32),
            vmem((ROWS, COLS), jnp.int32),
            vmem((WIN * WIN, ROWS, COLS), F32),
            vmem((EXTR, EXTC), F32),
            vmem((WIN, EXTR, COLS), F32),
            vmem((2, ROWS, HALF), F32),
            vmem((ROWS, HALF), F32),
            vmem((ROWS, HALF), F32),
            vmem((ROWS, HALF), F32),
            vmem((2, ROWS, HALF), F32),
            vmem((2, PADR, COLS), F32),
            vmem((2, ROWS, PADC), F32),
            vmem((2, 16, COLS), F32),
            vmem((2, 16, COLS), F32),
            vmem((4, 8, PADC), F32),
            vmem((BLOCKS, 8, PADC), F32),
            vmem((BLOCKS, 16, PADC), F32),
            vmem((BLOCKS * n_lon, 8, PADC), F32),
            vmem((BLOCKS * n_lon, 16, PADC), F32),
            pltpu.SMEM((1024,), jnp.int32),
            sems((9,)),
            sems((2 * N_SIDES,)),
            sems((2 * N_SIDES,)),
            sems((5,)),
            sems((5,)),
            sems((2, n_lon)),
            sems((2, n_lon)),
            pltpu.SemaphoreType.REGULAR,
        ],
        compiler_params=pltpu.CompilerParams(
            collective_id=0, has_side_effects=True, vmem_limit_bytes=32 * 2**20
        ),
    )(*[pltpu.with_memory_space_constraint(a, pltpu.HBM) for a in args])
    return pl.pallas_call(
        store,
        out_shape=tuple(jax.ShapeDtypeStruct(r.shape, r.dtype) for r in results),
        in_specs=[pl.BlockSpec(memory_space=pltpu.VMEM)] * 2,
        out_specs=(pl.BlockSpec(memory_space=pl.ANY),) * 2,
        scratch_shapes=[sems((2,))],
    )(*[pltpu.with_memory_space_constraint(r, pltpu.VMEM) for r in results])


def solution(mesh):
    placed = (
        P("comp", None, "lat", "lon"),
        P("comp", "lat", "lon"),
        P("comp", "lat", "lon"),
        P("lat", "lon"),
        P(None, "lat", "lon"),
        P(None, "lat", "lon"),
        P("lat", "lon"),
        P(),
    )
    return jax.shard_map(
        functools.partial(shards, mesh.shape["lon"], mesh.shape["lat"]),
        mesh=mesh,
        in_specs=placed,
        out_specs=(P("comp", None, "lat", "lon"), P("comp", "lat", "lon")),
        check_vma=False,
    )
```
